128 devices in a mesh: row: 16 (over z, y_hi, core), col: 8 (over y_lo, x).
Axes of the slice: x: 4, y: 4 (y_hi: 2, y_lo: 2; y = y_hi * 2 + y_lo), z: 4, core: 2. Of those that a mesh axis runs over, the one named last changes fastest.
Arguments:
- row_query: bfloat16 [512, 256, 768], P('row', 'col'), may hold values from -6 to 6
- row_key: bfloat16 [512, 256, 768], P('row', 'col'), may hold values from -6 to 6
- row_value: bfloat16 [512, 256, 768], P('row', 'col'), may hold values from -6 to 6
- row_out_grad: bfloat16 [512, 256, 768], P('row', 'col'), may hold values from -6 to 6
- col_query: bfloat16 [512, 256, 768], P('row', 'col'), may hold values from -6 to 6
- col_key: bfloat16 [512, 256, 768], P('row', 'col'), may hold values from -6 to 6
- col_value: bfloat16 [512, 256, 768], P('row', 'col'), may hold values from -6 to 6
- col_out_grad: bfloat16 [512, 256, 768], P('row', 'col'), may hold values from -6 to 6
Outputs:
- row_query_grad: bfloat16 [512, 256, 768], P('row', 'col')
- row_key_grad: bfloat16 [512, 256, 768], P('row', 'col')
- row_value_grad: bfloat16 [512, 256, 768], P('row', 'col')
- col_query_grad: bfloat16 [512, 256, 768], P('row', 'col')
- col_key_grad: bfloat16 [512, 256, 768], P('row', 'col')
- col_value_grad: bfloat16 [512, 256, 768], P('row', 'col')
The draws below stay inside these ranges and needn't reach their ends.
All inputs are finite; a program needn't handle non-finite values.
Results may differ from the reference program's by a relative error of at most 0.0086.
Values may be sent and summed in bfloat16 or wider, within the bound.
No kernel may reach another device: no remote copies, remote signals or barrier semaphores. Data moves between devices by JAX's collectives and lax.ppermute only.
A program may use at most 128 MiB of HBM per device.

```python
import math
import jax
import jax.numpy as jnp
from jax import lax

H = 12
HD = 64
D = 768
R = 512
C = 256


def normal_field(key, spread, bound):
    return jnp.clip(spread * jax.random.normal(key, (R, C, D), jnp.float32), -bound, bound)


def draw_row_query(key, part):
    key = jax.random.fold_in(key, 11)
    values = normal_field(key, 1.5, 6.0)
    return values.astype(jnp.bfloat16)


def draw_row_key(key, part):
    key = jax.random.fold_in(key, 12)
    values = normal_field(key, 1.5, 6.0)
    return values.astype(jnp.bfloat16)


def draw_col_query(key, part):
    key = jax.random.fold_in(key, 13)
    values = normal_field(key, 1.5, 6.0)
    return values.astype(jnp.bfloat16)


def draw_col_key(key, part):
    key = jax.random.fold_in(key, 14)
    values = normal_field(key, 1.5, 6.0)
    return values.astype(jnp.bfloat16)


def shard_levels(key, dims, cuts, low, high):
    factor_of, own = 1.0, jax.random.fold_in(key, 6)
    for axis_at, parts in cuts:
        heights = jnp.exp(jax.random.uniform(jax.random.fold_in(own, axis_at), (parts,), jnp.float32, low / len(cuts), high / len(cuts)))
        factor_of = factor_of * jnp.repeat(heights, dims[axis_at] // parts).reshape([-1 if axis == axis_at else 1 for axis in range(len(dims))])
    return factor_of


def scatter_about(stream_key, extent, width, most, pieces=(), held_as=jnp.bfloat16):
    drawn = jax.random.normal(stream_key, extent, jnp.float32) * width
    if len(pieces) > 0:
        drawn = shard_levels(stream_key, extent, pieces, -0.22, 0.18) * drawn
    return jnp.clip(drawn, min=-most, max=most).astype(held_as)


def setup_inputs(seed: int = 0) -> dict:
    streams_of = jax.random.split(jax.random.key(seed), 9)
    row_query = draw_row_query(jax.random.fold_in(streams_of[8], 71), 0)
    row_key = draw_row_key(jax.random.fold_in(streams_of[8], 71), 0)
    row_value = scatter_about(streams_of[2], (R, C, D), 1.0, 6.0, ((0, 16), (1, 8)))
    row_out_grad = scatter_about(streams_of[3], (R, C, D), 1.0, 6.0, ((0, 16), (1, 8)))
    col_query = draw_col_query(jax.random.fold_in(streams_of[8], 71), 0)
    col_key = draw_col_key(jax.random.fold_in(streams_of[8], 71), 0)
    col_value = scatter_about(streams_of[6], (R, C, D), 1.0, 6.0, ((0, 16), (1, 8)))
    col_out_grad = scatter_about(streams_of[7], (R, C, D), 1.0, 6.0, ((0, 16), (1, 8)))
    return dict(row_query=row_query, row_key=row_key, row_value=row_value, row_out_grad=row_out_grad, col_query=col_query, col_key=col_key, col_value=col_value, col_out_grad=col_out_grad)


def rounded(values):
    return lax.optimization_barrier(values.astype(jnp.bfloat16)).astype(jnp.float32)

def attention_softmax(logits, dprobs, factor):
    weights = jax.nn.softmax(logits * factor, axis=-1)
    slopes = weights * (dprobs - lax.optimization_barrier(jnp.sum(weights * dprobs, axis=-1, keepdims=True)))
    return (weights, slopes)

def tied_head(head_index, row_query, row_key, row_value, row_out_grad, factor):

    def take_head(tensor):
        return lax.dynamic_slice_in_dim(tensor, head_index * HD, HD, 2).astype(jnp.float32)
    queries = take_head(row_query)
    key_rows = take_head(row_key)
    value_rows = take_head(row_value)
    grad_rows = take_head(row_out_grad)
    logits = jnp.einsum('rid,rjd->ij', queries, key_rows)
    dprobs = jnp.einsum('rid,rjd->ij', grad_rows, value_rows)
    weights, slopes = attention_softmax(logits, dprobs, factor)
    query_grad = (factor * jnp.einsum('ij,rjd->rid', rounded(slopes), key_rows)).astype(jnp.bfloat16)
    key_grad = (factor * jnp.einsum('ij,rid->rjd', rounded(slopes), queries)).astype(jnp.bfloat16)
    value_grad = jnp.einsum('ij,rid->rjd', rounded(weights), grad_rows).astype(jnp.bfloat16)
    return (query_grad, key_grad, value_grad)

def joined_heads(stacked):
    moved = jnp.transpose(stacked, (1, 2, 0, 3))
    return moved.reshape(stacked.shape[1], stacked.shape[2], stacked.shape[0] * stacked.shape[3])

def column_one(inputs, factor):
    queries, key_rows, value_rows, grad_rows = [tensor.astype(jnp.float32).reshape(tensor.shape[0], H, HD) for tensor in inputs]
    logits = jnp.einsum('rhd,shd->hrs', queries, key_rows)
    dprobs = jnp.einsum('rhd,shd->hrs', grad_rows, value_rows)
    weights, slopes = attention_softmax(logits, dprobs, factor)
    query_grad = (factor * jnp.einsum('hrs,shd->rhd', rounded(slopes), key_rows)).astype(jnp.bfloat16)
    key_grad = (factor * jnp.einsum('hrs,rhd->shd', rounded(slopes), queries)).astype(jnp.bfloat16)
    value_grad = jnp.einsum('hrs,rhd->shd', rounded(weights), grad_rows).astype(jnp.bfloat16)
    total_rows = queries.shape[0]
    return (query_grad.reshape(total_rows, H * HD), key_grad.reshape(total_rows, H * HD), value_grad.reshape(total_rows, H * HD))

def reference(row_query, row_key, row_value, row_out_grad, col_query, col_key, col_value, col_out_grad):
    total_rows = row_query.shape[0]
    row_factor = 1.0 / math.sqrt(HD * total_rows)
    head_grads = lax.map(lambda head_index: tied_head(head_index, row_query, row_key, row_value, row_out_grad, row_factor), jnp.arange(H, dtype=jnp.int32))
    col_factor = 1.0 / math.sqrt(HD)
    by_column = tuple((jnp.transpose(tensor, (1, 0, 2)) for tensor in (col_query, col_key, col_value, col_out_grad)))
    column_grads = lax.map(lambda inputs: column_one(inputs, col_factor), by_column)
    return (joined_heads(head_grads[0]), joined_heads(head_grads[1]), joined_heads(head_grads[2]), jnp.transpose(column_grads[0], (1, 0, 2)), jnp.transpose(column_grads[1], (1, 0, 2)), jnp.transpose(column_grads[2], (1, 0, 2)))
```

```python
import functools
import math

import jax
import jax.numpy as jnp
from jax import lax
from jax.experimental import pallas as pl
from jax.experimental.pallas import tpu as pltpu
from jax.sharding import Mesh
from jax.sharding import PartitionSpec as P

H = 12
HD = 64
PAIR = 2 * HD
LOG2E = 1.4426950408889634
ROWS = ("z", "yh", "core")
VMEM = 48 * 1024 * 1024


def params():
    return pltpu.CompilerParams(vmem_limit_bytes=VMEM)


def nt(a, b):
    return lax.dot_general(a, b, (((1,), (1,)), ((), ())), preferred_element_type=jnp.float32)


def nn(a, b):
    return lax.dot_general(a, b, (((1,), (0,)), ((), ())), preferred_element_type=jnp.float32)


def column_kernel(x_ref, o_ref, *, chunk):
    groups, _, rows, width = x_ref.shape
    total = groups * rows
    query, key, value, grad = (x_ref[:, i].reshape(total, width) for i in range(4))
    low = lax.broadcasted_iota(jnp.int32, (total, width), 1) < HD
    zero = jnp.zeros_like(key)
    key_t = key.T
    scale = 1.0 / math.sqrt(HD)
    key_grads, value_grads, query_grads = [], [], []
    for head in range(2):
        keep = low if head == 0 else jnp.logical_not(low)
        key_h = jnp.where(keep, key, zero)
        value_h = jnp.where(keep, value, zero)
        key_th = key_t[head * HD : (head + 1) * HD]
        key_grad, value_grad, parts = None, None, []
        for at in range(0, total, chunk):
            query_c, grad_c = query[at : at + chunk], grad[at : at + chunk]
            logits = nt(key_h, query_c)
            dprobs = nt(value_h, grad_c)
            top = jnp.max(logits, axis=0, keepdims=True)
            probs = jnp.exp2((logits - top) * (scale * LOG2E))
            probs = probs * (1.0 / jnp.sum(probs, axis=0, keepdims=True))
            slopes = probs * (dprobs - jnp.sum(probs * dprobs, axis=0, keepdims=True))
            weights = probs.astype(jnp.bfloat16)
            slopes = slopes.astype(jnp.bfloat16)
            more_key, more_value = nn(slopes, query_c), nn(weights, grad_c)
            key_grad = more_key if key_grad is None else key_grad + more_key
            value_grad = more_value if value_grad is None else value_grad + more_value
            parts.append(nn(key_th, slopes))
        key_grads.append(key_grad)
        value_grads.append(value_grad)
        query_grads.append(jnp.concatenate(parts, axis=1))
    query_grad = jnp.concatenate(query_grads, axis=0).T * scale
    key_grad = jnp.where(low, key_grads[0], key_grads[1]) * scale
    value_grad = jnp.where(low, value_grads[0], value_grads[1])
    for i, grad in enumerate((query_grad, key_grad, value_grad)):
        o_ref[:, i] = grad.astype(jnp.bfloat16).reshape(groups, rows, width)


def column_backward(x, chunk=256):
    groups, _, rows, features = x.shape
    pairs = features // PAIR
    total = groups * rows
    return pl.pallas_call(
        functools.partial(column_kernel, chunk=chunk),
        grid=(pairs,),
        in_specs=[pl.BlockSpec((groups, 4, rows, PAIR), lambda i: (0, 0, 0, i))],
        out_specs=pl.BlockSpec((groups, 3, rows, PAIR), lambda i: (0, 0, 0, i)),
        out_shape=jax.ShapeDtypeStruct((groups, 3, rows, features), jnp.bfloat16),
        compiler_params=params(),
        cost_estimate=pl.CostEstimate(
            flops=20 * pairs * total * total * PAIR,
            bytes_accessed=14 * total * features,
            transcendentals=2 * pairs * total * total,
        ),
        name="column_attention",
    )(x)


def pack_kernel(*refs):
    ins, o_ref = refs[:-1], refs[-1]
    for i, ref in enumerate(ins):
        for r in range(0, ref.shape[0], 2):
            first, second = ref[r], ref[r + 1]
            lanes = slice(r * HD, r * HD + PAIR)
            o_ref[0, i, :, lanes] = jnp.concatenate([first[:, :HD], second[:, :HD]], axis=1)
            o_ref[1, i, :, lanes] = jnp.concatenate([first[:, HD:], second[:, HD:]], axis=1)


def pack_rows(*arrays):
    rows, columns, features = arrays[0].shape
    n = len(arrays)
    return pl.pallas_call(
        pack_kernel,
        grid=(features // PAIR,),
        in_specs=[pl.BlockSpec((rows, columns, PAIR), lambda i: (0, 0, i))] * n,
        out_specs=pl.BlockSpec((2, n, columns, rows * HD), lambda i: (i, 0, 0, 0)),
        out_shape=jax.ShapeDtypeStruct((features // HD, n, columns, rows * HD), jnp.bfloat16),
        compiler_params=params(),
        cost_estimate=pl.CostEstimate(
            flops=0, bytes_accessed=4 * n * rows * columns * features, transcendentals=0
        ),
        name="pack_rows",
    )(*arrays)


def unpack_kernel(x_ref, *o_refs):
    for i, ref in enumerate(o_refs):
        for r in range(0, ref.shape[0], 2):
            lanes = slice(r * HD, r * HD + PAIR)
            first, second = x_ref[0, i, :, lanes], x_ref[1, i, :, lanes]
            ref[r] = jnp.concatenate([first[:, :HD], second[:, :HD]], axis=1)
            ref[r + 1] = jnp.concatenate([first[:, HD:], second[:, HD:]], axis=1)


def unpack_rows(x):
    heads, n, columns, width = x.shape
    rows, features = width // HD, heads * HD
    return pl.pallas_call(
        unpack_kernel,
        grid=(heads // 2,),
        in_specs=[pl.BlockSpec((2, n, columns, width), lambda i: (i, 0, 0, 0))],
        out_specs=[pl.BlockSpec((rows, columns, PAIR), lambda i: (0, 0, i))] * n,
        out_shape=[jax.ShapeDtypeStruct((rows, columns, features), jnp.bfloat16)] * n,
        compiler_params=params(),
        cost_estimate=pl.CostEstimate(
            flops=0, bytes_accessed=4 * n * rows * columns * features, transcendentals=0
        ),
        name="unpack_rows",
    )(x)


def joined(refs, i):
    return jnp.concatenate([ref[0, i] for ref in refs], axis=0)


def logits_kernel(*refs, parts, slices):
    own, other, keys, o_ref = (
        refs[:parts],
        refs[parts : 2 * parts],
        refs[2 * parts : 3 * parts],
        refs[-1],
    )
    for i in range(2):
        right = joined(keys, i)
        for side, left in enumerate((own, other)):
            terms = nt(joined(left, i), right)
            o_ref[:, i, 0, side] = terms.reshape(slices, terms.shape[0] // slices, -1)


def tied_terms(own, other, keys, slices):
    parts = len(own)
    heads, _, columns, width = own[0].shape
    wide = parts * columns
    step = wide // slices
    return pl.pallas_call(
        functools.partial(logits_kernel, parts=parts, slices=slices),
        grid=(heads,),
        in_specs=[pl.BlockSpec((1, 2, columns, width), lambda i: (i, 0, 0, 0))] * (3 * parts),
        out_specs=pl.BlockSpec((slices, 2, 1, 2, step, wide), lambda i: (0, 0, i, 0, 0, 0)),
        out_shape=jax.ShapeDtypeStruct((slices, 2, heads, 2, step, wide), jnp.float32),
        compiler_params=params(),
        cost_estimate=pl.CostEstimate(
            flops=8 * heads * wide * wide * width,
            bytes_accessed=12 * heads * wide * width,
            transcendentals=0,
        ),
        name="tied_terms",
    )(*own, *other, *keys)


def grads_kernel(*refs, parts, factor):
    own, other, keys, other_keys = (refs[i * parts : (i + 1) * parts] for i in range(4))
    s_query, s_key, w_value, o_ref = refs[4 * parts :]
    results = (
        nn(s_query[0], jnp.concatenate([joined(keys, 0), joined(other_keys, 0)], axis=0)) * factor,
        nn(s_key[0], jnp.concatenate([joined(own, 0), joined(other, 0)], axis=0)) * factor,
        nn(w_value[0], jnp.concatenate([joined(own, 1), joined(other, 1)], axis=0)),
    )
    for i, result in enumerate(results):
        o_ref[:, 0, i] = result.astype(jnp.bfloat16).reshape(parts, -1, result.shape[1])


def tied_grads(own, other, keys, other_keys, s_query, s_key, w_value, factor):
    parts = len(own)
    heads, _, columns, width = own[0].shape
    wide = parts * columns
    two = pl.BlockSpec((1, 2, columns, width), lambda i: (i, 0, 0, 0))
    one = pl.BlockSpec((1, 1, columns, width), lambda i: (i, 0, 0, 0))
    square = pl.BlockSpec((1, wide, 2 * wide), lambda i: (i, 0, 0))
    return pl.pallas_call(
        functools.partial(grads_kernel, parts=parts, factor=factor),
        grid=(heads,),
        in_specs=[two] * (2 * parts) + [one] * (2 * parts) + [square] * 3,
        out_specs=pl.BlockSpec((parts, 1, 3, columns, width), lambda i: (0, i, 0, 0, 0)),
        out_shape=jax.ShapeDtypeStruct((parts, heads, 3, columns, width), jnp.bfloat16),
        compiler_params=params(),
        cost_estimate=pl.CostEstimate(
            flops=12 * heads * wide * wide * width,
            bytes_accessed=18 * heads * wide * width,
            transcendentals=0,
        ),
        name="tied_grads",
    )(*own, *other, *keys, *other_keys, s_query, s_key, w_value)


def shift(x, axis, by):
    n = lax.axis_size(axis)
    return lax.ppermute(x, axis, [(i, (i + by) % n) for i in range(n)])


def over_rows(x):
    return lax.all_to_all(x, ROWS, split_axis=0, concat_axis=0, tiled=True)


def column_in(arrays, piece, groups):
    stacked = jnp.stack([a[:, piece * groups : (piece + 1) * groups] for a in arrays])
    return over_rows(jnp.transpose(stacked, (2, 0, 1, 3)))


def local(row_query, row_key, row_value, row_out_grad, col_query, col_key, col_value, col_out_grad):
    groups = 1
    for axis in ROWS:
        groups *= lax.axis_size(axis)
    parts = lax.axis_size("x")
    here = lax.axis_index("x")
    rows, columns, features = row_query.shape
    row_factor = 1.0 / math.sqrt(HD * rows * groups)
    head_group = H // parts
    pieces = columns // groups

    def spread(packed):
        mine = [
            lax.dynamic_slice_in_dim(packed, head_group * ((here + s) % parts), head_group, 0)
            for s in range(parts)
        ]
        return [mine[0]] + [shift(mine[s], "x", s) for s in range(1, parts)]

    col_arrays = (col_query, col_key, col_value, col_out_grad)
    col_parts = [column_in(col_arrays, p, groups) for p in range(pieces)]

    own = spread(pack_rows(row_query, row_out_grad))
    other = [shift(c, "yl", 1) for c in own]
    keys = spread(pack_rows(row_key, row_value))
    other_keys = [shift(c[:, :1], "yl", 1) for c in keys]

    terms = over_rows(tied_terms(own, other, keys, groups))
    sums = jnp.sum(terms, axis=0)
    across = shift(sums[:, :, 1], "yl", 1)
    logits, dprobs = jnp.concatenate([sums[:, :, 0], across], axis=-1)
    probs = jax.nn.softmax(logits * row_factor, axis=-1)
    slopes = probs * (dprobs - jnp.sum(probs * dprobs, axis=-1, keepdims=True))
    both = jnp.stack([slopes, probs]).astype(jnp.bfloat16)
    wide = both.shape[-1] // 2
    crossed = shift(both[..., wide:], "yl", 1)
    payload = jnp.concatenate([both[..., :wide], both[:1, ..., wide:], crossed], axis=0)
    whole = over_rows(jnp.broadcast_to(payload[None], (groups,) + payload.shape))
    whole = jnp.transpose(whole, (1, 2, 0, 3, 4)).reshape(5, head_group, wide, wide)
    s_own, w_own, s_right, s_below, w_below = whole
    s_query = jnp.concatenate([s_own, s_right], axis=-1)
    s_key = jnp.swapaxes(jnp.concatenate([s_own, s_below], axis=1), 1, 2)
    w_value = jnp.swapaxes(jnp.concatenate([w_own, w_below], axis=1), 1, 2)

    grads = tied_grads(own, other, keys, other_keys, s_query, s_key, w_value, row_factor)
    gathered = jnp.zeros((H, 3, columns, rows * HD), jnp.bfloat16)
    for s in range(parts):
        piece = grads[s] if s == 0 else shift(grads[s], "x", parts - s)
        gathered = lax.dynamic_update_slice_in_dim(
            gathered, piece, head_group * ((here + s) % parts), 0
        )
    row_grads = unpack_rows(gathered)

    col_back = [over_rows(column_backward(p)) for p in col_parts]
    col_grads = [
        jnp.concatenate([jnp.transpose(p[:, i], (1, 0, 2)) for p in col_back], axis=1)
        for i in range(3)
    ]
    return (*row_grads, *col_grads)


def solution(mesh):
    split = Mesh(mesh.devices.reshape(4, 2, 2, 2, 4), ("z", "yh", "core", "yl", "x"))
    spec = P(ROWS, ("yl", "x"), None)
    return jax.shard_map(
        local, mesh=split, in_specs=(spec,) * 8, out_specs=(spec,) * 6, check_vma=False
    )
```

```python
import functools
import math

import jax
import jax.numpy as jnp
from jax import lax
from jax.experimental import pallas as pl
from jax.experimental.pallas import tpu as pltpu
from jax.sharding import Mesh
from jax.sharding import PartitionSpec as P

H = 12
HD = 64
PAIR = 2 * HD
WIDE = 3 * PAIR
LOG2E = 1.4426950408889634
ROWS = ("z", "yh", "core")
VMEM = 48 * 1024 * 1024
VMEM_ALL = 60 * 1024 * 1024
COST = pl.CostEstimate(flops=1, bytes_accessed=1, transcendentals=0)


def params(limit=VMEM):
    return pltpu.CompilerParams(vmem_limit_bytes=limit)


def nt(a, b):
    return lax.dot_general(a, b, (((1,), (1,)), ((), ())), preferred_element_type=jnp.float32)


def nn(a, b):
    return lax.dot_general(a, b, (((1,), (0,)), ((), ())), preferred_element_type=jnp.float32)


def tn(a, b):
    return lax.dot_general(a, b, (((0,), (0,)), ((), ())), preferred_element_type=jnp.float32)


def column_kernel(x_ref, o_ref, *, chunk):
    groups, _, rows, width = x_ref.shape
    total = groups * rows
    query, key, value, grad = (x_ref[:, i].reshape(total, width) for i in range(4))
    low = lax.broadcasted_iota(jnp.int32, (total, width), 1) < HD
    zero = jnp.zeros_like(key)
    key_t = key.T
    scale = 1.0 / math.sqrt(HD)
    key_grads, value_grads, query_grads = [], [], []
    for head in range(2):
        keep = low if head == 0 else jnp.logical_not(low)
        key_h = jnp.where(keep, key, zero)
        value_h = jnp.where(keep, value, zero)
        key_th = key_t[head * HD : (head + 1) * HD]
        key_grad, value_grad, parts = None, None, []
        for at in range(0, total, chunk):
            query_c, grad_c = query[at : at + chunk], grad[at : at + chunk]
            logits = nt(key_h, query_c)
            dprobs = nt(value_h, grad_c)
            top = jnp.max(logits, axis=0, keepdims=True)
            probs = jnp.exp2((logits - top) * (scale * LOG2E))
            probs = probs * (1.0 / jnp.sum(probs, axis=0, keepdims=True))
            slopes = probs * (dprobs - jnp.sum(probs * dprobs, axis=0, keepdims=True))
            weights = probs.astype(jnp.bfloat16)
            slopes = slopes.astype(jnp.bfloat16)
            more_key, more_value = nn(slopes, query_c), nn(weights, grad_c)
            key_grad = more_key if key_grad is None else key_grad + more_key
            value_grad = more_value if value_grad is None else value_grad + more_value
            parts.append(nn(key_th, slopes))
        key_grads.append(key_grad)
        value_grads.append(value_grad)
        query_grads.append(jnp.concatenate(parts, axis=1))
    query_grad = jnp.concatenate(query_grads, axis=0).T * scale
    key_grad = jnp.where(low, key_grads[0], key_grads[1]) * scale
    value_grad = jnp.where(low, value_grads[0], value_grads[1])
    for i, grad in enumerate((query_grad, key_grad, value_grad)):
        o_ref[:, i] = grad.astype(jnp.bfloat16).reshape(groups, rows, width)


def column_backward(x, pieces, chunk=256):
    groups, _, rows, features = x.shape
    pairs, total = features // PAIR, groups * rows
    return pl.pallas_call(
        functools.partial(column_kernel, chunk=chunk),
        grid=(pieces, pairs),
        in_specs=[pl.BlockSpec((groups, 4, rows, PAIR), lambda p, i: (0, p, 0, i))],
        out_specs=pl.BlockSpec((groups, 3, rows, PAIR), lambda p, i: (0, p, 0, i)),
        out_shape=jax.ShapeDtypeStruct((groups, 3 * pieces, rows, features), jnp.bfloat16),
        compiler_params=params(),
        cost_estimate=pl.CostEstimate(
            flops=20 * pieces * pairs * total * total * PAIR,
            bytes_accessed=14 * pieces * total * features,
            transcendentals=2 * pieces * pairs * total * total,
        ),
        name="column_attention",
    )(x)


def pack_kernel(here_ref, *refs, parts):
    ins, outs, held, sems = refs[: -parts - 2], refs[-parts - 2 : -2], refs[-2], refs[-1]
    group = held.shape[1]
    for t in range(parts):
        for k in range(group):
            lanes = slice((t * group + k) * HD, (t * group + k + 1) * HD)
            for i, ref in enumerate(ins):
                for r in range(0, ref.shape[0], 2):
                    held[t, k, i, :, r * HD : r * HD + PAIR] = jnp.concatenate(
                        [ref[r, :, lanes], ref[r + 1, :, lanes]], axis=1
                    )
        for s, out in enumerate(outs):

            @pl.when(lax.rem(t + parts - here_ref[0], parts) == s)
            def _(t=t, out=out):
                pltpu.make_async_copy(held.at[t], out, sems.at[t]).start()

    for t in range(parts):
        pltpu.make_async_copy(held.at[t], outs[0], sems.at[t]).wait()


def pack_rows(here, parts, *arrays):
    rows, columns, features = arrays[0].shape
    n, group = len(arrays), features // HD // parts
    shape = (group, n, columns, rows * HD)
    return pl.pallas_call(
        functools.partial(pack_kernel, parts=parts),
        in_specs=[pl.BlockSpec(memory_space=pltpu.SMEM)]
        + [pl.BlockSpec(memory_space=pltpu.VMEM)] * n,
        out_specs=[pl.BlockSpec(memory_space=pl.ANY)] * parts,
        out_shape=[jax.ShapeDtypeStruct(shape, jnp.bfloat16)] * parts,
        scratch_shapes=[
            pltpu.VMEM((parts,) + shape, jnp.bfloat16),
            pltpu.SemaphoreType.DMA((parts,)),
        ],
        compiler_params=params(),
        cost_estimate=COST,
        name="pack_rows",
    )(here, *arrays)


def unpack_kernel(here_ref, *refs, parts):
    ins, o_refs, held, sems = refs[:parts], refs[parts:-2], refs[-2], refs[-1]
    group = held.shape[1]
    for t in range(parts):
        for s, ref in enumerate(ins):

            @pl.when(lax.rem(t + parts - here_ref[0], parts) == s)
            def _(t=t, ref=ref):
                pltpu.make_async_copy(ref, held.at[t], sems.at[t]).start()

    for t in range(parts):
        pltpu.make_async_copy(ins[0], held.at[t], sems.at[t]).wait()
    for head in range(0, parts * group, 2):
        lanes = slice(head * HD, head * HD + PAIR)
        even, odd = divmod(head, group), divmod(head + 1, group)
        for i, ref in enumerate(o_refs):
            for r in range(0, ref.shape[0], 2):
                span = slice(r * HD, r * HD + PAIR)
                first, second = held[*even, i, :, span], held[*odd, i, :, span]
                ref[r, :, lanes] = jnp.concatenate([first[:, :HD], second[:, :HD]], axis=1)
                ref[r + 1, :, lanes] = jnp.concatenate([first[:, HD:], second[:, HD:]], axis=1)


def unpack_rows(here, chunks):
    parts = len(chunks)
    group, n, columns, width = chunks[0].shape
    rows, features = width // HD, parts * group * HD
    return pl.pallas_call(
        functools.partial(unpack_kernel, parts=parts),
        in_specs=[pl.BlockSpec(memory_space=pltpu.SMEM)]
        + [pl.BlockSpec(memory_space=pl.ANY)] * parts,
        out_specs=[pl.BlockSpec(memory_space=pltpu.VMEM)] * n,
        out_shape=[jax.ShapeDtypeStruct((rows, columns, features), jnp.bfloat16)] * n,
        scratch_shapes=[
            pltpu.VMEM((parts,) + chunks[0].shape, jnp.bfloat16),
            pltpu.SemaphoreType.DMA((parts,)),
        ],
        compiler_params=params(),
        cost_estimate=COST,
        name="unpack_rows",
    )(here, *chunks)


def joined(refs, i):
    return jnp.concatenate([ref[0, i] for ref in refs], axis=0)


def logits_kernel(*refs, parts, slices):
    own, other, keys, values = (refs[i * parts : (i + 1) * parts] for i in range(4))
    o_ref = refs[-1]
    for i in range(2):
        right = joined(values if i else keys, 0)
        for side, left in enumerate((own, other)):
            terms = nt(joined(left, i), right)
            o_ref[:, i, 0, side] = terms.reshape(slices, terms.shape[0] // slices, -1)


def tied_terms(own, other, keys, values, slices):
    parts = len(own)
    heads, _, columns, width = own[0].shape
    wide = parts * columns
    step = wide // slices
    return pl.pallas_call(
        functools.partial(logits_kernel, parts=parts, slices=slices),
        grid=(heads,),
        in_specs=[pl.BlockSpec((1, 2, columns, width), lambda i: (i, 0, 0, 0))] * (2 * parts)
        + [pl.BlockSpec((1, 1, columns, width), lambda i: (i, 0, 0, 0))] * (2 * parts),
        out_specs=pl.BlockSpec((slices, 2, 1, 2, step, wide), lambda i: (0, 0, i, 0, 0, 0)),
        out_shape=jax.ShapeDtypeStruct((slices, 2, heads, 2, step, wide), jnp.float32),
        compiler_params=params(VMEM_ALL),
        cost_estimate=COST,
        name="tied_terms",
    )(*own, *other, *keys, *values)


def grads_kernel(*refs, parts, factor):
    own, other, keys, other_keys = (refs[i * parts : (i + 1) * parts] for i in range(4))
    tied_ref, outs = refs[4 * parts], refs[4 * parts + 1 :]
    s_own, w_own, s_right, s_below, w_below = (tied_ref[i, 0] for i in range(5))
    s_query = jnp.concatenate([s_own, s_right], axis=1)
    s_key = jnp.concatenate([s_own, s_below], axis=0)
    w_value = jnp.concatenate([w_own, w_below], axis=0)
    results = (
        nn(s_query, jnp.concatenate([joined(keys, 0), joined(other_keys, 0)], axis=0)) * factor,
        tn(s_key, jnp.concatenate([joined(own, 0), joined(other, 0)], axis=0)) * factor,
        tn(w_value, jnp.concatenate([joined(own, 1), joined(other, 1)], axis=0)),
    )
    for i, result in enumerate(results):
        result = result.astype(jnp.bfloat16)
        for s, out in enumerate(outs):
            out[0, i] = result[s * out.shape[2] : (s + 1) * out.shape[2]]


def tied_grads(own, other, keys, other_keys, tied, factor):
    parts = len(own)
    heads, _, columns, width = own[0].shape
    wide = parts * columns
    two = pl.BlockSpec((1, 2, columns, width), lambda i: (i, 0, 0, 0))
    one = pl.BlockSpec((1, 1, columns, width), lambda i: (i, 0, 0, 0))
    square = pl.BlockSpec((5, 1, wide, wide), lambda i: (0, i, 0, 0))
    return pl.pallas_call(
        functools.partial(grads_kernel, parts=parts, factor=factor),
        grid=(heads,),
        in_specs=[two] * (2 * parts) + [one] * (2 * parts) + [square],
        out_specs=[pl.BlockSpec((1, 3, columns, width), lambda i: (i, 0, 0, 0))] * parts,
        out_shape=[jax.ShapeDtypeStruct((heads, 3, columns, width), jnp.bfloat16)] * parts,
        compiler_params=params(VMEM_ALL),
        cost_estimate=COST,
        name="tied_grads",
    )(*own, *other, *keys, *other_keys, tied)


def shift(x, axis, by):
    n = lax.axis_size(axis)
    return lax.ppermute(x, axis, [(i, (i + by) % n) for i in range(n)])


def over_rows(x):
    return lax.all_to_all(x, ROWS, split_axis=0, concat_axis=0, tiled=True)


def after(x, *others):
    return lax.optimization_barrier((x, others))[0]


def turned(x):
    outer, inner, width = x.shape
    n = outer * inner
    to = lax.broadcasted_iota(jnp.int32, (n, n), 0)
    source = lax.broadcasted_iota(jnp.int32, (n, n), 1)
    turn = jnp.where(source == (to % outer) * inner + to // outer, 1.0, 0.0).astype(x.dtype)
    return nn(turn, x.reshape(n, width)).astype(x.dtype).reshape(inner, outer, width)


def column_pack_kernel(*refs):
    ins, o_ref = refs[:-1], refs[-1]
    groups, _, rows, _ = o_ref.shape
    for i, ref in enumerate(ins):
        for r in range(0, rows, groups):
            o_ref[:, i, r : r + groups] = turned(ref[r : r + groups])


def column_pack(arrays, pieces, groups):
    rows, _, features = arrays[0].shape
    n = len(arrays)
    return pl.pallas_call(
        column_pack_kernel,
        grid=(pieces, features // WIDE),
        in_specs=[pl.BlockSpec((rows, groups, WIDE), lambda p, i: (0, p, i))] * n,
        out_specs=pl.BlockSpec((groups, n, rows, WIDE), lambda p, i: (0, p, 0, i)),
        out_shape=jax.ShapeDtypeStruct((groups, n * pieces, rows, features), jnp.bfloat16),
        compiler_params=params(),
        cost_estimate=COST,
        name="column_pack",
    )(*arrays)


def column_unpack_kernel(x_ref, *o_refs):
    groups, _, rows, _ = x_ref.shape
    for i, ref in enumerate(o_refs):
        for r in range(0, rows, groups):
            ref[r : r + groups] = turned(x_ref[:, i, r : r + groups])


def column_unpack(x, pieces):
    groups, parts, rows, features = x.shape
    n = parts // pieces
    return pl.pallas_call(
        column_unpack_kernel,
        grid=(pieces, features // WIDE),
        in_specs=[pl.BlockSpec((groups, n, rows, WIDE), lambda p, i: (0, p, 0, i))],
        out_specs=[pl.BlockSpec((rows, groups, WIDE), lambda p, i: (0, p, i))] * n,
        out_shape=[jax.ShapeDtypeStruct((rows, pieces * groups, features), jnp.bfloat16)] * n,
        compiler_params=params(),
        cost_estimate=COST,
        name="column_unpack",
    )(x)


def local(row_query, row_key, row_value, row_out_grad, col_query, col_key, col_value, col_out_grad):
    groups = 1
    for axis in ROWS:
        groups *= lax.axis_size(axis)
    parts = lax.axis_size("x")
    here = lax.axis_index("x")
    rows, columns, features = row_query.shape
    row_factor = 1.0 / math.sqrt(HD * rows * groups)
    head_group = H // parts
    pieces = columns // groups

    def spread(chunks):
        return [chunks[0]] + [shift(chunks[s], "x", s) for s in range(1, parts)]

    here = jnp.reshape(here, (1,)).astype(jnp.int32)
    col_ready = column_pack((col_query, col_key, col_value, col_out_grad), pieces, groups)
    col_in = over_rows(col_ready)

    row_arrays = after((row_query, row_out_grad, row_key, row_value), col_ready)
    own = spread(pack_rows(here, parts, *row_arrays[:2]))
    keys = spread(pack_rows(here, parts, row_arrays[2]))
    values = spread(pack_rows(here, parts, row_arrays[3]))
    other = [shift(c, "yl", 1) for c in own]
    col_done = column_backward(col_in, pieces)

    other_keys = [shift(c, "yl", 1) for c in after(keys[:2], other[-2])]
    terms = tied_terms(*after((own, other, keys, values), col_done), groups)
    terms = over_rows(after(terms, other_keys[0]))
    sums = jnp.sum(after(terms, other_keys), axis=0)
    across = shift(sums, "yl", 1)
    other_keys += [shift(c, "yl", 1) for c in after(keys[2:], across)]

    logits, dprobs = jnp.concatenate([sums, jnp.flip(across, 2)], axis=-1)
    probs = jax.nn.softmax(logits * row_factor, axis=-1)
    slopes = probs * (dprobs - jnp.sum(probs * dprobs, axis=-1, keepdims=True))
    probs, slopes = probs.astype(jnp.bfloat16), slopes.astype(jnp.bfloat16)
    wide = probs.shape[-1] // 2
    payload = jnp.stack(
        [
            slopes[:, 0, :, :wide],
            probs[:, 0, :, :wide],
            slopes[:, 0, :, wide:],
            slopes[:, 1, :, :wide],
            probs[:, 1, :, :wide],
        ]
    )
    whole = over_rows(jnp.broadcast_to(payload[None], (groups,) + payload.shape))
    col_grads = column_unpack(over_rows(after(col_done, whole, other_keys)), pieces)
    whole = jnp.transpose(whole, (1, 2, 0, 3, 4)).reshape(5, head_group, wide, wide)
    grads = tied_grads(own, other, keys, other_keys, whole, row_factor)
    chunks = [grads[0]] + [shift(grads[s], "x", parts - s) for s in range(1, parts)]
    row_grads = unpack_rows(here, chunks)
    return (*row_grads, *col_grads)


def solution(mesh):
    split = Mesh(mesh.devices.reshape(4, 2, 2, 2, 4), ("z", "yh", "core", "yl", "x"))
    spec = P(ROWS, ("yl", "x"), None)
    return jax.shard_map(
        local, mesh=split, in_specs=(spec,) * 8, out_specs=(spec,) * 6, check_vma=False
    )
```

```python
import functools
import math

import jax
import jax.numpy as jnp
from jax import lax
from jax.experimental import pallas as pl
from jax.experimental.pallas import tpu as pltpu
from jax.sharding import Mesh
from jax.sharding import PartitionSpec as P

H = 12
HD = 64
PAIR = 2 * HD
LOG2E = 1.4426950408889634
ROWS = ("z", "yh", "core")
VMEM = 48 * 1024 * 1024
VMEM_ALL = 60 * 1024 * 1024
COST = pl.CostEstimate(flops=1, bytes_accessed=1, transcendentals=0)


def params(limit=VMEM):
    return pltpu.CompilerParams(vmem_limit_bytes=limit)


def nt(a, b):
    return lax.dot_general(a, b, (((1,), (1,)), ((), ())), preferred_element_type=jnp.float32)


def nn(a, b):
    return lax.dot_general(a, b, (((1,), (0,)), ((), ())), preferred_element_type=jnp.float32)


def tn(a, b):
    return lax.dot_general(a, b, (((0,), (0,)), ((), ())), preferred_element_type=jnp.float32)


def column_kernel(x_ref, o_ref, *, chunk):
    groups, _, rows, width = x_ref.shape
    total = groups * rows
    query, key, value, grad = (x_ref[:, i].reshape(total, width) for i in range(4))
    low = lax.broadcasted_iota(jnp.int32, (total, width), 1) < HD
    zero = jnp.zeros_like(key)
    key_t = key.T
    scale = 1.0 / math.sqrt(HD)
    key_grads, value_grads, query_grads = [], [], []
    for head in range(2):
        keep = low if head == 0 else jnp.logical_not(low)
        key_h = jnp.where(keep, key, zero)
        value_h = jnp.where(keep, value, zero)
        key_th = key_t[head * HD : (head + 1) * HD]
        key_grad, value_grad, parts = None, None, []
        for at in range(0, total, chunk):
            query_c, grad_c = query[at : at + chunk], grad[at : at + chunk]
            logits = nt(key_h, query_c)
            dprobs = nt(value_h, grad_c)
            top = jnp.max(logits, axis=0, keepdims=True)
            probs = jnp.exp2((logits - top) * (scale * LOG2E))
            probs = probs * (1.0 / jnp.sum(probs, axis=0, keepdims=True))
            slopes = probs * (dprobs - jnp.sum(probs * dprobs, axis=0, keepdims=True))
            weights = probs.astype(jnp.bfloat16)
            slopes = slopes.astype(jnp.bfloat16)
            more_key, more_value = nn(slopes, query_c), nn(weights, grad_c)
            key_grad = more_key if key_grad is None else key_grad + more_key
            value_grad = more_value if value_grad is None else value_grad + more_value
            parts.append(nn(key_th, slopes))
        key_grads.append(key_grad)
        value_grads.append(value_grad)
        query_grads.append(jnp.concatenate(parts, axis=1))
    query_grad = jnp.concatenate(query_grads, axis=0).T * scale
    key_grad = jnp.where(low, key_grads[0], key_grads[1]) * scale
    value_grad = jnp.where(low, value_grads[0], value_grads[1])
    for i, grad in enumerate((query_grad, key_grad, value_grad)):
        o_ref[:, i] = grad.astype(jnp.bfloat16).reshape(groups, rows, width)


def column_backward(x, pieces, chunk=512):
    groups, _, rows, features = x.shape
    pairs, total = features // PAIR, groups * rows
    return pl.pallas_call(
        functools.partial(column_kernel, chunk=chunk),
        grid=(pieces, pairs),
        in_specs=[pl.BlockSpec((groups, 4, rows, PAIR), lambda p, i: (0, p, 0, i))],
        out_specs=pl.BlockSpec((groups, 3, rows, PAIR), lambda p, i: (0, p, 0, i)),
        out_shape=jax.ShapeDtypeStruct((groups, 3 * pieces, rows, features), jnp.bfloat16),
        compiler_params=params(),
        cost_estimate=pl.CostEstimate(
            flops=20 * pieces * pairs * total * total * PAIR,
            bytes_accessed=14 * pieces * total * features,
            transcendentals=2 * pieces * pairs * total * total,
        ),
        name="column_attention",
    )(x)


def pack_kernel(here_ref, *refs, parts):
    ins, outs, held, sems = refs[: -parts - 2], refs[-parts - 2 : -2], refs[-2], refs[-1]
    group = held.shape[1]
    for t in range(parts):
        for k in range(group):
            lanes = slice((t * group + k) * HD, (t * group + k + 1) * HD)
            for i, ref in enumerate(ins):
                for r in range(0, ref.shape[0], 2):
                    held[t, k, i, :, r * HD : r * HD + PAIR] = jnp.concatenate(
                        [ref[r, :, lanes], ref[r + 1, :, lanes]], axis=1
                    )
        for s, out in enumerate(outs):

            @pl.when(lax.rem(t + parts - here_ref[0], parts) == s)
            def _(t=t, out=out):
                pltpu.make_async_copy(held.at[t], out, sems.at[t]).start()

    for t in range(parts):
        pltpu.make_async_copy(held.at[t], outs[0], sems.at[t]).wait()


def pack_rows(here, parts, *arrays):
    rows, columns, features = arrays[0].shape
    n, group = len(arrays), features // HD // parts
    shape = (group, n, columns, rows * HD)
    return pl.pallas_call(
        functools.partial(pack_kernel, parts=parts),
        in_specs=[pl.BlockSpec(memory_space=pltpu.SMEM)]
        + [pl.BlockSpec(memory_space=pltpu.VMEM)] * n,
        out_specs=[pl.BlockSpec(memory_space=pl.ANY)] * parts,
        out_shape=[jax.ShapeDtypeStruct(shape, jnp.bfloat16)] * parts,
        scratch_shapes=[
            pltpu.VMEM((parts,) + shape, jnp.bfloat16),
            pltpu.SemaphoreType.DMA((parts,)),
        ],
        compiler_params=params(),
        cost_estimate=COST,
        name="pack_rows",
    )(here, *arrays)


def unpack_kernel(here_ref, *refs, parts):
    ins, o_refs, held, sems = refs[:parts], refs[parts:-2], refs[-2], refs[-1]
    group = held.shape[1]
    for t in range(parts):
        for s, ref in enumerate(ins):

            @pl.when(lax.rem(t + parts - here_ref[0], parts) == s)
            def _(t=t, ref=ref):
                pltpu.make_async_copy(ref, held.at[t], sems.at[t]).start()

    for t in range(parts):
        pltpu.make_async_copy(ins[0], held.at[t], sems.at[t]).wait()
    for head in range(0, parts * group, 2):
        lanes = slice(head * HD, head * HD + PAIR)
        even, odd = divmod(head, group), divmod(head + 1, group)
        for i, ref in enumerate(o_refs):
            for r in range(0, ref.shape[0], 2):
                span = slice(r * HD, r * HD + PAIR)
                first, second = held[*even, i, :, span], held[*odd, i, :, span]
                ref[r, :, lanes] = jnp.concatenate([first[:, :HD], second[:, :HD]], axis=1)
                ref[r + 1, :, lanes] = jnp.concatenate([first[:, HD:], second[:, HD:]], axis=1)


def unpack_rows(here, chunks):
    parts = len(chunks)
    group, n, columns, width = chunks[0].shape
    rows, features = width // HD, parts * group * HD
    return pl.pallas_call(
        functools.partial(unpack_kernel, parts=parts),
        in_specs=[pl.BlockSpec(memory_space=pltpu.SMEM)]
        + [pl.BlockSpec(memory_space=pl.ANY)] * parts,
        out_specs=[pl.BlockSpec(memory_space=pltpu.VMEM)] * n,
        out_shape=[jax.ShapeDtypeStruct((rows, columns, features), jnp.bfloat16)] * n,
        scratch_shapes=[
            pltpu.VMEM((parts,) + chunks[0].shape, jnp.bfloat16),
            pltpu.SemaphoreType.DMA((parts,)),
        ],
        compiler_params=params(),
        cost_estimate=COST,
        name="unpack_rows",
    )(here, *chunks)


def joined(refs, i):
    return jnp.concatenate([ref[0, i] for ref in refs], axis=0)


def terms_kernel(*refs, parts):
    left, keys, values = (refs[i * parts : (i + 1) * parts] for i in range(3))
    o_ref = refs[-1]
    for i, right in enumerate((keys, values)):
        terms = nt(joined(left, i), joined(right, 0))
        o_ref[:, i, 0, 0] = terms.reshape(o_ref.shape[0], -1, terms.shape[1])


def tied_terms(left, keys, values, slices, side, held=()):
    parts = len(left)
    heads, _, columns, width = left[0].shape
    wide = parts * columns
    step = wide // slices
    return pl.pallas_call(
        functools.partial(terms_kernel, parts=parts),
        grid=(heads,),
        in_specs=[pl.BlockSpec((1, 2, columns, width), lambda i: (i, 0, 0, 0))] * parts
        + [pl.BlockSpec((1, 1, columns, width), lambda i: (i, 0, 0, 0))] * (2 * parts)
        + [pl.BlockSpec(memory_space=pl.ANY)] * len(held),
        out_specs=pl.BlockSpec(
            (slices, 2, 1, 1, step, wide), lambda i: (0, 0, i, side, 0, 0)
        ),
        out_shape=jax.ShapeDtypeStruct((slices, 2, heads, 2, step, wide), jnp.float32),
        input_output_aliases={3 * parts: 0} if held else {},
        compiler_params=params(VMEM_ALL),
        cost_estimate=COST,
        name="tied_terms",
    )(*left, *keys, *values, *held)


def pair_grads_kernel(*refs, parts, factor):
    own, other, (tied_ref, *outs) = refs[:parts], refs[parts : 2 * parts], refs[2 * parts :]
    s_own, w_own, _, s_below, w_below = (tied_ref[i, 0] for i in range(5))
    s_key = jnp.concatenate([s_own, s_below], axis=0)
    w_value = jnp.concatenate([w_own, w_below], axis=0)
    results = (
        tn(s_key, jnp.concatenate([joined(own, 0), joined(other, 0)], axis=0)) * factor,
        tn(w_value, jnp.concatenate([joined(own, 1), joined(other, 1)], axis=0)),
    )
    for i, result in enumerate(results):
        result = result.astype(jnp.bfloat16)
        for s, out in enumerate(outs[i * parts : (i + 1) * parts]):
            out[0, 0] = result[s * out.shape[2] : (s + 1) * out.shape[2]]


def query_grads_kernel(*refs, parts, factor):
    keys, other_keys, (tied_ref, *outs) = refs[:parts], refs[parts : 2 * parts], refs[2 * parts :]
    s_query = jnp.concatenate([tied_ref[0, 0], tied_ref[2, 0]], axis=1)
    result = nn(s_query, jnp.concatenate([joined(keys, 0), joined(other_keys, 0)], axis=0))
    result = (result * factor).astype(jnp.bfloat16)
    for s, out in enumerate(outs):
        out[0, 0] = result[s * out.shape[2] : (s + 1) * out.shape[2]]


def tied_grads(kernel, own, other, tied, factor, name):
    parts = len(own)
    heads, n, columns, width = own[0].shape
    wide = parts * columns
    chunk = pl.BlockSpec((1, n, columns, width), lambda i: (i, 0, 0, 0))
    one = pl.BlockSpec((1, 1, columns, width), lambda i: (i, 0, 0, 0))
    square = pl.BlockSpec((5, 1, wide, wide), lambda i: (0, i, 0, 0))
    return pl.pallas_call(
        functools.partial(kernel, parts=parts, factor=factor),
        grid=(heads,),
        in_specs=[chunk] * (2 * parts) + [square],
        out_specs=[one] * (n * parts),
        out_shape=[jax.ShapeDtypeStruct((heads, 1, columns, width), jnp.bfloat16)] * (n * parts),
        compiler_params=params(VMEM_ALL),
        cost_estimate=COST,
        name=name,
    )(*own, *other, tied)


def shift(x, axis, by):
    n = lax.axis_size(axis)
    return lax.ppermute(x, axis, [(i, (i + by) % n) for i in range(n)])


def over_rows(x):
    return lax.all_to_all(x, ROWS, split_axis=0, concat_axis=0, tiled=True)


def after(x, *others):
    return lax.optimization_barrier((x, others))[0]


def turned(x):
    outer, inner, width = x.shape
    n = outer * inner
    to = lax.broadcasted_iota(jnp.int32, (n, n), 0)
    source = lax.broadcasted_iota(jnp.int32, (n, n), 1)
    turn = jnp.where(source == (to % outer) * inner + to // outer, 1.0, 0.0).astype(x.dtype)
    return nn(turn, x.reshape(n, width)).astype(x.dtype).reshape(inner, outer, width)


def column_pack_kernel(*refs):
    ins, o_ref = refs[:-1], refs[-1]
    groups, _, rows, _ = o_ref.shape
    for i, ref in enumerate(ins):
        for r in range(0, rows, groups):
            o_ref[:, i, r : r + groups] = turned(ref[r : r + groups])


def column_pack(arrays, pieces, groups):
    rows, _, features = arrays[0].shape
    n = len(arrays)
    return pl.pallas_call(
        column_pack_kernel,
        grid=(pieces,),
        in_specs=[pl.BlockSpec((rows, groups, features), lambda p: (0, p, 0))] * n,
        out_specs=pl.BlockSpec((groups, n, rows, features), lambda p: (0, p, 0, 0)),
        out_shape=jax.ShapeDtypeStruct((groups, n * pieces, rows, features), jnp.bfloat16),
        compiler_params=params(VMEM_ALL),
        cost_estimate=COST,
        name="column_pack",
    )(*arrays)


def column_unpack_kernel(x_ref, *o_refs):
    groups, _, rows, _ = x_ref.shape
    for i, ref in enumerate(o_refs):
        for r in range(0, rows, groups):
            ref[r : r + groups] = turned(x_ref[:, i, r : r + groups])


def column_unpack(x, pieces):
    groups, parts, rows, features = x.shape
    n = parts // pieces
    return pl.pallas_call(
        column_unpack_kernel,
        grid=(pieces,),
        in_specs=[pl.BlockSpec((groups, n, rows, features), lambda p: (0, p, 0, 0))],
        out_specs=[pl.BlockSpec((rows, groups, features), lambda p: (0, p, 0))] * n,
        out_shape=[jax.ShapeDtypeStruct((rows, pieces * groups, features), jnp.bfloat16)] * n,
        compiler_params=params(),
        cost_estimate=COST,
        name="column_unpack",
    )(x)


def local(row_query, row_key, row_value, row_out_grad, col_query, col_key, col_value, col_out_grad):
    groups = 1
    for axis in ROWS:
        groups *= lax.axis_size(axis)
    parts = lax.axis_size("x")
    here = lax.axis_index("x")
    rows, columns, features = row_query.shape
    row_factor = 1.0 / math.sqrt(HD * rows * groups)
    head_group = H // parts
    pieces = columns // groups

    def spread(chunks):
        return [chunks[0]] + [shift(chunks[s], "x", s) for s in range(1, parts)]

    here = jnp.reshape(here, (1,)).astype(jnp.int32)
    col_ready = column_pack((col_query, col_key, col_value, col_out_grad), pieces, groups)
    col_in = over_rows(col_ready)

    row_arrays = after((row_query, row_out_grad, row_key, row_value), col_ready)
    own = spread(pack_rows(here, parts, *row_arrays[:2]))
    keys = spread(pack_rows(here, parts, row_arrays[2]))
    values = spread(pack_rows(here, parts, row_arrays[3]))
    other = [shift(c, "yl", 1) for c in own]
    half = tied_terms(own, keys, values, groups, 0)
    col_done = column_backward(after(col_in, half), pieces)

    def across(keys, *others):
        return [shift(c, "yl", 1) for c in after(keys, others)]

    other_keys = across(keys[:2], other[-2])
    left, half = after((other, half), col_done)
    terms = tied_terms(left, keys, values, groups, 1, (half,))
    terms = over_rows(after(terms, other_keys[0]))
    sums = jnp.sum(after(terms, other_keys[1]), axis=0)
    swapped = shift(sums, "yl", 1)
    late = across([jnp.concatenate(keys[2:])], swapped)[0]
    other_keys += [late[at : at + head_group] for at in range(0, late.shape[0], head_group)]

    logits, dprobs = jnp.concatenate([sums, jnp.flip(swapped, 2)], axis=-1)
    probs = jax.nn.softmax(logits * row_factor, axis=-1)
    slopes = probs * (dprobs - jnp.sum(probs * dprobs, axis=-1, keepdims=True))
    probs, slopes = probs.astype(jnp.bfloat16), slopes.astype(jnp.bfloat16)
    wide = probs.shape[-1] // 2
    payload = jnp.stack(
        [
            slopes[:, 0, :, :wide],
            probs[:, 0, :, :wide],
            slopes[:, 0, :, wide:],
            slopes[:, 1, :, :wide],
            probs[:, 1, :, :wide],
        ]
    )
    whole = over_rows(jnp.broadcast_to(payload[None], (groups,) + payload.shape))
    whole = jnp.transpose(whole, (1, 2, 0, 3, 4)).reshape(5, head_group, wide, wide)
    def back(chunks):
        return [chunks[0]] + [shift(chunks[s], "x", parts - s) for s in range(1, parts)]

    pair_grads = tied_grads(pair_grads_kernel, own, other, whole, row_factor, "pair_grads")
    key_chunks, value_chunks = back(pair_grads[:parts]), back(pair_grads[parts:])
    col_grads = column_unpack(over_rows(after(col_done, whole, late)), pieces)
    keys = after(keys, value_chunks[1])
    query_grads = tied_grads(query_grads_kernel, keys, other_keys, whole, row_factor, "query_grads")
    chunks = (back(query_grads), key_chunks, value_chunks)
    row_grads = [unpack_rows(here, c)[0] for c in chunks]

    return (*row_grads, *col_grads)


def solution(mesh):
    split = Mesh(mesh.devices.reshape(4, 2, 2, 2, 4), ("z", "yh", "core", "yl", "x"))
    spec = P(ROWS, ("yl", "x"), None)
    return jax.shard_map(
        local, mesh=split, in_specs=(spec,) * 8, out_specs=(spec,) * 6, check_vma=False
    )
```

```python
import functools
import math

import jax
import jax.numpy as jnp
from jax import lax
from jax.experimental import pallas as pl
from jax.experimental.pallas import tpu as pltpu
from jax.sharding import Mesh
from jax.sharding import PartitionSpec as P

H = 12
HD = 64
PAIR = 2 * HD
LOG2E = 1.4426950408889634
ROWS = ("z", "yh", "core")
VMEM = 48 * 1024 * 1024
VMEM_ALL = 60 * 1024 * 1024
COST = pl.CostEstimate(flops=1, bytes_accessed=1, transcendentals=0)


def params(limit=VMEM):
    return pltpu.CompilerParams(vmem_limit_bytes=limit)


def nt(a, b):
    return lax.dot_general(a, b, (((1,), (1,)), ((), ())), preferred_element_type=jnp.float32)


def nn(a, b):
    return lax.dot_general(a, b, (((1,), (0,)), ((), ())), preferred_element_type=jnp.float32)


def tn(a, b):
    return lax.dot_general(a, b, (((0,), (0,)), ((), ())), preferred_element_type=jnp.float32)


def column_kernel(x_ref, o_ref, *, chunk):
    groups, _, rows, width = x_ref.shape
    total = groups * rows
    query, key, value, grad = (x_ref[:, i].reshape(total, width) for i in range(4))
    low = lax.broadcasted_iota(jnp.int32, (total, width), 1) < HD
    zero = jnp.zeros_like(key)
    key_t = key.T
    scale = 1.0 / math.sqrt(HD)
    key_grads, value_grads, query_grads = [], [], []
    for head in range(2):
        keep = low if head == 0 else jnp.logical_not(low)
        key_h = jnp.where(keep, key, zero)
        value_h = jnp.where(keep, value, zero)
        key_th = key_t[head * HD : (head + 1) * HD]
        key_grad, value_grad, parts = None, None, []
        for at in range(0, total, chunk):
            query_c, grad_c = query[at : at + chunk], grad[at : at + chunk]
            logits = nt(key_h, query_c)
            dprobs = nt(value_h, grad_c)
            top = jnp.max(logits, axis=0, keepdims=True)
            probs = jnp.exp2((logits - top) * (scale * LOG2E))
            probs = probs * (1.0 / jnp.sum(probs, axis=0, keepdims=True))
            slopes = probs * (dprobs - jnp.sum(probs * dprobs, axis=0, keepdims=True))
            weights = probs.astype(jnp.bfloat16)
            slopes = slopes.astype(jnp.bfloat16)
            more_key, more_value = nn(slopes, query_c), nn(weights, grad_c)
            key_grad = more_key if key_grad is None else key_grad + more_key
            value_grad = more_value if value_grad is None else value_grad + more_value
            parts.append(nn(key_th, slopes))
        key_grads.append(key_grad)
        value_grads.append(value_grad)
        query_grads.append(jnp.concatenate(parts, axis=1))
    query_grad = jnp.concatenate(query_grads, axis=0).T * scale
    key_grad = jnp.where(low, key_grads[0], key_grads[1]) * scale
    value_grad = jnp.where(low, value_grads[0], value_grads[1])
    for i, grad in enumerate((query_grad, key_grad, value_grad)):
        o_ref[:, i] = grad.astype(jnp.bfloat16).reshape(groups, rows, width)


def column_backward(x, pieces, chunk=512):
    groups, _, rows, features = x.shape
    pairs, total = features // PAIR, groups * rows
    return pl.pallas_call(
        functools.partial(column_kernel, chunk=chunk),
        grid=(pieces, pairs),
        in_specs=[pl.BlockSpec((groups, 4, rows, PAIR), lambda p, i: (0, p, 0, i))],
        out_specs=pl.BlockSpec((groups, 3, rows, PAIR), lambda p, i: (0, p, 0, i)),
        out_shape=jax.ShapeDtypeStruct((groups, 3 * pieces, rows, features), jnp.bfloat16),
        compiler_params=params(),
        cost_estimate=pl.CostEstimate(
            flops=20 * pieces * pairs * total * total * PAIR,
            bytes_accessed=14 * pieces * total * features,
            transcendentals=2 * pieces * pairs * total * total,
        ),
        name="column_attention",
    )(x)


def pack_kernel(here_ref, *refs, parts):
    ins, outs, held, sems = refs[: -parts - 2], refs[-parts - 2 : -2], refs[-2], refs[-1]
    group = held.shape[1]
    for t in range(parts):
        for k in range(group):
            lanes = slice((t * group + k) * HD, (t * group + k + 1) * HD)
            for i, ref in enumerate(ins):
                for r in range(0, ref.shape[0], 2):
                    held[t, k, i, :, r * HD : r * HD + PAIR] = jnp.concatenate(
                        [ref[r, :, lanes], ref[r + 1, :, lanes]], axis=1
                    )
        for s, out in enumerate(outs):

            @pl.when(lax.rem(t + parts - here_ref[0], parts) == s)
            def _(t=t, out=out):
                pltpu.make_async_copy(held.at[t], out, sems.at[t]).start()

    for t in range(parts):
        pltpu.make_async_copy(held.at[t], outs[0], sems.at[t]).wait()


def pack_rows(here, parts, *arrays):
    rows, columns, features = arrays[0].shape
    n, group = len(arrays), features // HD // parts
    shape = (group, n, columns, rows * HD)
    return pl.pallas_call(
        functools.partial(pack_kernel, parts=parts),
        in_specs=[pl.BlockSpec(memory_space=pltpu.SMEM)]
        + [pl.BlockSpec(memory_space=pltpu.VMEM)] * n,
        out_specs=[pl.BlockSpec(memory_space=pl.ANY)] * parts,
        out_shape=[jax.ShapeDtypeStruct(shape, jnp.bfloat16)] * parts,
        scratch_shapes=[
            pltpu.VMEM((parts,) + shape, jnp.bfloat16),
            pltpu.SemaphoreType.DMA((parts,)),
        ],
        compiler_params=params(),
        cost_estimate=COST,
        name="pack_rows",
    )(here, *arrays)


def unpack_kernel(here_ref, *refs, parts):
    ins, o_refs, held, sems = refs[:parts], refs[parts:-2], refs[-2], refs[-1]
    group = held.shape[1]
    for t in range(parts):
        for s, ref in enumerate(ins):

            @pl.when(lax.rem(t + parts - here_ref[0], parts) == s)
            def _(t=t, ref=ref):
                pltpu.make_async_copy(ref, held.at[t], sems.at[t]).start()

    for t in range(parts):
        pltpu.make_async_copy(ins[0], held.at[t], sems.at[t]).wait()
    for head in range(0, parts * group, 2):
        lanes = slice(head * HD, head * HD + PAIR)
        even, odd = divmod(head, group), divmod(head + 1, group)
        for i, ref in enumerate(o_refs):
            for r in range(0, ref.shape[0], 2):
                span = slice(r * HD, r * HD + PAIR)
                first, second = held[*even, i, :, span], held[*odd, i, :, span]
                ref[r, :, lanes] = jnp.concatenate([first[:, :HD], second[:, :HD]], axis=1)
                ref[r + 1, :, lanes] = jnp.concatenate([first[:, HD:], second[:, HD:]], axis=1)


def unpack_rows(here, chunks):
    parts = len(chunks)
    group, n, columns, width = chunks[0].shape
    rows, features = width // HD, parts * group * HD
    return pl.pallas_call(
        functools.partial(unpack_kernel, parts=parts),
        in_specs=[pl.BlockSpec(memory_space=pltpu.SMEM)]
        + [pl.BlockSpec(memory_space=pl.ANY)] * parts,
        out_specs=[pl.BlockSpec(memory_space=pltpu.VMEM)] * n,
        out_shape=[jax.ShapeDtypeStruct((rows, columns, features), jnp.bfloat16)] * n,
        scratch_shapes=[
            pltpu.VMEM((parts,) + chunks[0].shape, jnp.bfloat16),
            pltpu.SemaphoreType.DMA((parts,)),
        ],
        compiler_params=params(),
        cost_estimate=COST,
        name="unpack_rows",
    )(here, *chunks)


def joined(refs, i):
    return jnp.concatenate([ref[0, i] for ref in refs], axis=0)


def terms_kernel(*refs, parts):
    left, keys, values = (refs[i * parts : (i + 1) * parts] for i in range(3))
    o_ref = refs[-1]
    for i, right in enumerate((keys, values)):
        terms = nt(joined(left, i), joined(right, 0))
        o_ref[:, i, 0, 0] = terms.reshape(o_ref.shape[0], -1, terms.shape[1])


def tied_terms(left, keys, values, slices, side, held=()):
    parts = len(left)
    heads, _, columns, width = left[0].shape
    wide = parts * columns
    step = wide // slices
    return pl.pallas_call(
        functools.partial(terms_kernel, parts=parts),
        grid=(heads,),
        in_specs=[pl.BlockSpec((1, 2, columns, width), lambda i: (i, 0, 0, 0))] * parts
        + [pl.BlockSpec((1, 1, columns, width), lambda i: (i, 0, 0, 0))] * (2 * parts)
        + [pl.BlockSpec(memory_space=pl.ANY)] * len(held),
        out_specs=pl.BlockSpec(
            (slices, 2, 1, 1, step, wide), lambda i: (0, 0, i, side, 0, 0)
        ),
        out_shape=jax.ShapeDtypeStruct((slices, 2, heads, 2, step, wide), jnp.float32),
        input_output_aliases={3 * parts: 0} if held else {},
        compiler_params=params(VMEM_ALL),
        cost_estimate=COST,
        name="tied_terms",
    )(*left, *keys, *values, *held)


def pair_grads_kernel(*refs, parts, factor):
    own, other, (tied_ref, *outs) = refs[:parts], refs[parts : 2 * parts], refs[2 * parts :]
    s_own, w_own, _, s_below, w_below = (tied_ref[i, 0] for i in range(5))
    s_key = jnp.concatenate([s_own, s_below], axis=0)
    w_value = jnp.concatenate([w_own, w_below], axis=0)
    results = (
        tn(s_key, jnp.concatenate([joined(own, 0), joined(other, 0)], axis=0)) * factor,
        tn(w_value, jnp.concatenate([joined(own, 1), joined(other, 1)], axis=0)),
    )
    for i, result in enumerate(results):
        result = result.astype(jnp.bfloat16)
        for s, out in enumerate(outs[i * parts : (i + 1) * parts]):
            out[0, 0] = result[s * out.shape[2] : (s + 1) * out.shape[2]]


def query_grads_kernel(*refs, parts, factor):
    keys, other_keys, (tied_ref, *outs) = refs[:parts], refs[parts : 2 * parts], refs[2 * parts :]
    s_query = jnp.concatenate([tied_ref[0, 0], tied_ref[2, 0]], axis=1)
    result = nn(s_query, jnp.concatenate([joined(keys, 0), joined(other_keys, 0)], axis=0))
    result = (result * factor).astype(jnp.bfloat16)
    for s, out in enumerate(outs):
        out[0, 0] = result[s * out.shape[2] : (s + 1) * out.shape[2]]


def tied_grads(kernel, own, other, tied, factor, name):
    parts = len(own)
    heads, n, columns, width = own[0].shape
    wide = parts * columns
    chunk = pl.BlockSpec((1, n, columns, width), lambda i: (i, 0, 0, 0))
    one = pl.BlockSpec((1, 1, columns, width), lambda i: (i, 0, 0, 0))
    square = pl.BlockSpec((5, 1, wide, wide), lambda i: (0, i, 0, 0))
    return pl.pallas_call(
        functools.partial(kernel, parts=parts, factor=factor),
        grid=(heads,),
        in_specs=[chunk] * (2 * parts) + [square],
        out_specs=[one] * (n * parts),
        out_shape=[jax.ShapeDtypeStruct((heads, 1, columns, width), jnp.bfloat16)] * (n * parts),
        compiler_params=params(VMEM_ALL),
        cost_estimate=COST,
        name=name,
    )(*own, *other, tied)


def shift(x, axis, by):
    n = lax.axis_size(axis)
    return lax.ppermute(x, axis, [(i, (i + by) % n) for i in range(n)])


def over_rows(x):
    return lax.all_to_all(x, ROWS, split_axis=0, concat_axis=0, tiled=True)


def after(x, *others):
    return lax.optimization_barrier((x, others))[0]


def turned(x):
    outer, inner, width = x.shape
    n = outer * inner
    to = lax.broadcasted_iota(jnp.int32, (n, n), 0)
    source = lax.broadcasted_iota(jnp.int32, (n, n), 1)
    turn = jnp.where(source == (to % outer) * inner + to // outer, 1.0, 0.0).astype(x.dtype)
    return nn(turn, x.reshape(n, width)).astype(x.dtype).reshape(inner, outer, width)


def column_pack_kernel(*refs):
    ins, o_ref = refs[:-1], refs[-1]
    groups, _, rows, _ = o_ref.shape
    for i, ref in enumerate(ins):
        for r in range(0, rows, groups):
            o_ref[:, i, r : r + groups] = turned(ref[r : r + groups])


def column_pack(arrays, pieces, groups):
    rows, _, features = arrays[0].shape
    n = len(arrays)
    return pl.pallas_call(
        column_pack_kernel,
        grid=(pieces,),
        in_specs=[pl.BlockSpec((rows, groups, features), lambda p: (0, p, 0))] * n,
        out_specs=pl.BlockSpec((groups, n, rows, features), lambda p: (0, p, 0, 0)),
        out_shape=jax.ShapeDtypeStruct((groups, n * pieces, rows, features), jnp.bfloat16),
        compiler_params=params(VMEM_ALL),
        cost_estimate=COST,
        name="column_pack",
    )(*arrays)


def column_unpack_kernel(x_ref, *o_refs):
    groups, _, rows, _ = x_ref.shape
    for i, ref in enumerate(o_refs):
        for r in range(0, rows, groups):
            ref[r : r + groups] = turned(x_ref[:, i, r : r + groups])


def column_unpack(x, pieces):
    groups, parts, rows, features = x.shape
    n = parts // pieces
    return pl.pallas_call(
        column_unpack_kernel,
        grid=(pieces,),
        in_specs=[pl.BlockSpec((groups, n, rows, features), lambda p: (0, p, 0, 0))],
        out_specs=[pl.BlockSpec((rows, groups, features), lambda p: (0, p, 0))] * n,
        out_shape=[jax.ShapeDtypeStruct((rows, pieces * groups, features), jnp.bfloat16)] * n,
        compiler_params=params(),
        cost_estimate=COST,
        name="column_unpack",
    )(x)


def local(row_query, row_key, row_value, row_out_grad, col_query, col_key, col_value, col_out_grad):
    groups = 1
    for axis in ROWS:
        groups *= lax.axis_size(axis)
    parts = lax.axis_size("x")
    here = lax.axis_index("x")
    rows, columns, features = row_query.shape
    row_factor = 1.0 / math.sqrt(HD * rows * groups)
    head_group = H // parts
    pieces = columns // groups

    def spread(chunks):
        return [chunks[0]] + [shift(chunks[s], "x", s) for s in range(1, parts)]

    here = jnp.reshape(here, (1,)).astype(jnp.int32)
    col_ready = column_pack((col_query, col_key, col_value, col_out_grad), pieces, groups)
    col_in = over_rows(col_ready)

    row_arrays = after((row_query, row_out_grad, row_key, row_value), col_ready)
    own = spread(pack_rows(here, parts, *row_arrays[:2]))
    keys = spread(pack_rows(here, parts, row_arrays[2]))
    values = spread(pack_rows(here, parts, row_arrays[3]))
    other = [shift(c, "yl", 1) for c in own]
    half = tied_terms(own, keys, values, groups, 0)
    col_done = column_backward(after(col_in, half), pieces)

    def across(keys, *others):
        return [shift(c, "yl", 1) for c in after(keys, others)]

    early = across([jnp.concatenate(keys[:2])], other[-2])[0]
    left, half = after((other, half), col_done)
    terms = over_rows(tied_terms(left, keys, values, groups, 1, (half,)))
    sums = jnp.sum(after(terms, early), axis=0)
    swapped = shift(sums, "yl", 1)
    late = across([jnp.concatenate(keys[2:])], swapped)[0]
    other_keys = [
        part[at : at + head_group]
        for part in (early, late)
        for at in range(0, part.shape[0], head_group)
    ]

    logits, dprobs = jnp.concatenate([sums, jnp.flip(swapped, 2)], axis=-1)
    probs = jax.nn.softmax(logits * row_factor, axis=-1)
    slopes = probs * (dprobs - jnp.sum(probs * dprobs, axis=-1, keepdims=True))
    probs, slopes = probs.astype(jnp.bfloat16), slopes.astype(jnp.bfloat16)
    wide = probs.shape[-1] // 2
    payload = jnp.stack(
        [
            slopes[:, 0, :, :wide],
            probs[:, 0, :, :wide],
            slopes[:, 0, :, wide:],
            slopes[:, 1, :, :wide],
            probs[:, 1, :, :wide],
        ]
    )
    whole = over_rows(jnp.broadcast_to(payload[None], (groups,) + payload.shape))
    whole = jnp.transpose(whole, (1, 2, 0, 3, 4)).reshape(5, head_group, wide, wide)
    def back(chunks):
        return [chunks[0]] + [shift(chunks[s], "x", parts - s) for s in range(1, parts)]

    pair_grads = tied_grads(pair_grads_kernel, own, other, whole, row_factor, "pair_grads")
    key_chunks, value_chunks = back(pair_grads[:parts]), back(pair_grads[parts:])
    col_grads = column_unpack(over_rows(after(col_done, whole, late)), pieces)
    keys = after(keys, value_chunks[1])
    query_grads = tied_grads(query_grads_kernel, keys, other_keys, whole, row_factor, "query_grads")
    chunks = (back(query_grads), key_chunks, value_chunks)
    row_grads = [unpack_rows(here, c)[0] for c in chunks[1:]]
    row_grads.insert(0, unpack_rows(here, after(chunks[0], col_grads))[0])

    return (*row_grads, *col_grads)


def solution(mesh):
    split = Mesh(mesh.devices.reshape(4, 2, 2, 2, 4), ("z", "yh", "core", "yl", "x"))
    spec = P(ROWS, ("yl", "x"), None)
    return jax.shard_map(
        local, mesh=split, in_specs=(spec,) * 8, out_specs=(spec,) * 6, check_vma=False
    )
```

```python
import functools
import math

import jax
import jax.numpy as jnp
from jax import lax
from jax.experimental import pallas as pl
from jax.experimental.pallas import tpu as pltpu
from jax.sharding import Mesh
from jax.sharding import PartitionSpec as P

H = 12
HD = 64
PAIR = 2 * HD
LOG2E = 1.4426950408889634
ROWS = ("z", "yh", "core")
VMEM = 48 * 1024 * 1024
VMEM_ALL = 60 * 1024 * 1024
COST = pl.CostEstimate(flops=1, bytes_accessed=1, transcendentals=0)


def params(limit=VMEM):
    return pltpu.CompilerParams(vmem_limit_bytes=limit)


def nt(a, b):
    return lax.dot_general(a, b, (((1,), (1,)), ((), ())), preferred_element_type=jnp.float32)


def nn(a, b):
    return lax.dot_general(a, b, (((1,), (0,)), ((), ())), preferred_element_type=jnp.float32)


def tn(a, b):
    return lax.dot_general(a, b, (((0,), (0,)), ((), ())), preferred_element_type=jnp.float32)


def column_kernel(x_ref, o_ref, *, chunk):
    groups, _, rows, width = x_ref.shape
    total = groups * rows
    query, key, value, grad = (x_ref[:, i].reshape(total, width) for i in range(4))
    low = lax.broadcasted_iota(jnp.int32, (total, width), 1) < HD
    zero = jnp.zeros_like(key)
    key_t = key.T
    scale = 1.0 / math.sqrt(HD)
    key_grads, value_grads, query_grads = [], [], []
    for head in range(2):
        keep = low if head == 0 else jnp.logical_not(low)
        key_h = jnp.where(keep, key, zero)
        value_h = jnp.where(keep, value, zero)
        key_th = key_t[head * HD : (head + 1) * HD]
        key_grad, value_grad, parts = None, None, []
        for at in range(0, total, chunk):
            query_c, grad_c = query[at : at + chunk], grad[at : at + chunk]
            logits = nt(key_h, query_c)
            dprobs = nt(value_h, grad_c)
            top = jnp.max(logits, axis=0, keepdims=True)
            probs = jnp.exp2((logits - top) * (scale * LOG2E))
            probs = probs * (1.0 / jnp.sum(probs, axis=0, keepdims=True))
            slopes = probs * (dprobs - jnp.sum(probs * dprobs, axis=0, keepdims=True))
            weights = probs.astype(jnp.bfloat16)
            slopes = slopes.astype(jnp.bfloat16)
            more_key, more_value = nn(slopes, query_c), nn(weights, grad_c)
            key_grad = more_key if key_grad is None else key_grad + more_key
            value_grad = more_value if value_grad is None else value_grad + more_value
            parts.append(nn(key_th, slopes))
        key_grads.append(key_grad)
        value_grads.append(value_grad)
        query_grads.append(jnp.concatenate(parts, axis=1))
    query_grad = jnp.concatenate(query_grads, axis=0).T * scale
    key_grad = jnp.where(low, key_grads[0], key_grads[1]) * scale
    value_grad = jnp.where(low, value_grads[0], value_grads[1])
    for i, grad in enumerate((query_grad, key_grad, value_grad)):
        o_ref[:, i] = grad.astype(jnp.bfloat16).reshape(groups, rows, width)


def column_backward(x, pieces, chunk=512):
    groups, _, rows, features = x.shape
    pairs, total = features // PAIR, groups * rows
    return pl.pallas_call(
        functools.partial(column_kernel, chunk=chunk),
        grid=(pieces, pairs),
        in_specs=[pl.BlockSpec((groups, 4, rows, PAIR), lambda p, i: (0, p, 0, i))],
        out_specs=pl.BlockSpec((groups, 3, rows, PAIR), lambda p, i: (0, p, 0, i)),
        out_shape=jax.ShapeDtypeStruct((groups, 3 * pieces, rows, features), jnp.bfloat16),
        compiler_params=params(),
        cost_estimate=pl.CostEstimate(
            flops=20 * pieces * pairs * total * total * PAIR,
            bytes_accessed=14 * pieces * total * features,
            transcendentals=2 * pieces * pairs * total * total,
        ),
        name="column_attention",
    )(x)


def pack_kernel(here_ref, *refs, parts):
    ins, outs, held, sems = refs[: -parts - 2], refs[-parts - 2 : -2], refs[-2], refs[-1]
    group = held.shape[1]
    for t in range(parts):
        for k in range(group):
            lanes = slice((t * group + k) * HD, (t * group + k + 1) * HD)
            for i, ref in enumerate(ins):
                for r in range(0, ref.shape[0], 2):
                    held[t, k, i, :, r * HD : r * HD + PAIR] = jnp.concatenate(
                        [ref[r, :, lanes], ref[r + 1, :, lanes]], axis=1
                    )
        for s, out in enumerate(outs):

            @pl.when(lax.rem(t + parts - here_ref[0], parts) == s)
            def _(t=t, out=out):
                pltpu.make_async_copy(held.at[t], out, sems.at[t]).start()

    for t in range(parts):
        pltpu.make_async_copy(held.at[t], outs[0], sems.at[t]).wait()


def pack_rows(here, parts, *arrays):
    rows, columns, features = arrays[0].shape
    n, group = len(arrays), features // HD // parts
    shape = (group, n, columns, rows * HD)
    return pl.pallas_call(
        functools.partial(pack_kernel, parts=parts),
        in_specs=[pl.BlockSpec(memory_space=pltpu.SMEM)]
        + [pl.BlockSpec(memory_space=pltpu.VMEM)] * n,
        out_specs=[pl.BlockSpec(memory_space=pl.ANY)] * parts,
        out_shape=[jax.ShapeDtypeStruct(shape, jnp.bfloat16)] * parts,
        scratch_shapes=[
            pltpu.VMEM((parts,) + shape, jnp.bfloat16),
            pltpu.SemaphoreType.DMA((parts,)),
        ],
        compiler_params=params(),
        cost_estimate=COST,
        name="pack_rows",
    )(here, *arrays)


def unpack_kernel(here_ref, *refs, parts):
    ins, o_refs, held, sems = refs[:parts], refs[parts:-2], refs[-2], refs[-1]
    group = held.shape[1]
    for t in range(parts):
        for s, ref in enumerate(ins):

            @pl.when(lax.rem(t + parts - here_ref[0], parts) == s)
            def _(t=t, ref=ref):
                pltpu.make_async_copy(ref, held.at[t], sems.at[t]).start()

    for t in range(parts):
        pltpu.make_async_copy(ins[0], held.at[t], sems.at[t]).wait()
    for head in range(0, parts * group, 2):
        lanes = slice(head * HD, head * HD + PAIR)
        even, odd = divmod(head, group), divmod(head + 1, group)
        for i, ref in enumerate(o_refs):
            for r in range(0, ref.shape[0], 2):
                span = slice(r * HD, r * HD + PAIR)
                first, second = held[*even, i, :, span], held[*odd, i, :, span]
                ref[r, :, lanes] = jnp.concatenate([first[:, :HD], second[:, :HD]], axis=1)
                ref[r + 1, :, lanes] = jnp.concatenate([first[:, HD:], second[:, HD:]], axis=1)


def unpack_rows(here, chunks):
    parts = len(chunks)
    group, n, columns, width = chunks[0].shape
    rows, features = width // HD, parts * group * HD
    return pl.pallas_call(
        functools.partial(unpack_kernel, parts=parts),
        in_specs=[pl.BlockSpec(memory_space=pltpu.SMEM)]
        + [pl.BlockSpec(memory_space=pl.ANY)] * parts,
        out_specs=[pl.BlockSpec(memory_space=pltpu.VMEM)] * n,
        out_shape=[jax.ShapeDtypeStruct((rows, columns, features), jnp.bfloat16)] * n,
        scratch_shapes=[
            pltpu.VMEM((parts,) + chunks[0].shape, jnp.bfloat16),
            pltpu.SemaphoreType.DMA((parts,)),
        ],
        compiler_params=params(),
        cost_estimate=COST,
        name="unpack_rows",
    )(here, *chunks)


def joined(refs, i):
    return jnp.concatenate([ref[0, i] for ref in refs], axis=0)


def terms_kernel(*refs, count, parts):
    left, keys, values = refs[:count], refs[count : count + parts], refs[count + parts :][:parts]
    o_ref = refs[-1]
    for i, right in enumerate((keys, values)):
        terms = nt(joined(left, i), joined(right, 0))
        o_ref[:, i, 0, 0] = terms.reshape(o_ref.shape[0], -1, terms.shape[1])


def tied_terms(left, keys, values, slices, side, first=0, held=()):
    parts, count = len(keys), len(left)
    heads, _, columns, width = left[0].shape
    wide = parts * columns
    step, span = wide // slices, slices * count // parts
    return pl.pallas_call(
        functools.partial(terms_kernel, count=count, parts=parts),
        grid=(heads,),
        in_specs=[pl.BlockSpec((1, 2, columns, width), lambda i: (i, 0, 0, 0))] * count
        + [pl.BlockSpec((1, 1, columns, width), lambda i: (i, 0, 0, 0))] * (2 * parts)
        + [pl.BlockSpec(memory_space=pl.ANY)] * len(held),
        out_specs=pl.BlockSpec(
            (span, 2, 1, 1, step, wide), lambda i: (first // count, 0, i, side, 0, 0)
        ),
        out_shape=jax.ShapeDtypeStruct((slices, 2, heads, 2, step, wide), jnp.float32),
        input_output_aliases={count + 2 * parts: 0} if held else {},
        compiler_params=params(VMEM_ALL),
        cost_estimate=COST,
        name="tied_terms",
    )(*left, *keys, *values, *held)


def pair_grads_kernel(*refs, parts, factor):
    own, other, (tied_ref, *outs) = refs[:parts], refs[parts : 2 * parts], refs[2 * parts :]
    s_own, w_own, _, s_below, w_below = (tied_ref[i, 0] for i in range(5))
    s_key = jnp.concatenate([s_own, s_below], axis=0)
    w_value = jnp.concatenate([w_own, w_below], axis=0)
    results = (
        tn(s_key, jnp.concatenate([joined(own, 0), joined(other, 0)], axis=0)) * factor,
        tn(w_value, jnp.concatenate([joined(own, 1), joined(other, 1)], axis=0)),
    )
    for i, result in enumerate(results):
        result = result.astype(jnp.bfloat16)
        for s, out in enumerate(outs[i * parts : (i + 1) * parts]):
            out[0, 0] = result[s * out.shape[2] : (s + 1) * out.shape[2]]


def query_grads_kernel(*refs, parts, factor):
    keys, other_keys, (tied_ref, *outs) = refs[:parts], refs[parts : 2 * parts], refs[2 * parts :]
    s_query = jnp.concatenate([tied_ref[0, 0], tied_ref[2, 0]], axis=1)
    result = nn(s_query, jnp.concatenate([joined(keys, 0), joined(other_keys, 0)], axis=0))
    result = (result * factor).astype(jnp.bfloat16)
    for s, out in enumerate(outs):
        out[0, 0] = result[s * out.shape[2] : (s + 1) * out.shape[2]]


def tied_grads(kernel, own, other, tied, factor, name):
    parts = len(own)
    heads, n, columns, width = own[0].shape
    places = [
        pl.BlockSpec((1, n, columns, width), lambda i, at=at: (at + i, 0, 0, 0))
        for x in other
        for at in range(0, x.shape[0], heads)
    ]
    other = [x for x in other for _ in range(0, x.shape[0], heads)]
    wide = parts * columns
    chunk = pl.BlockSpec((1, n, columns, width), lambda i: (i, 0, 0, 0))
    one = pl.BlockSpec((1, 1, columns, width), lambda i: (i, 0, 0, 0))
    square = pl.BlockSpec((5, 1, wide, wide), lambda i: (0, i, 0, 0))
    return pl.pallas_call(
        functools.partial(kernel, parts=parts, factor=factor),
        grid=(heads,),
        in_specs=[chunk] * parts + places + [square],
        out_specs=[one] * (n * parts),
        out_shape=[jax.ShapeDtypeStruct((heads, 1, columns, width), jnp.bfloat16)] * (n * parts),
        compiler_params=params(VMEM_ALL),
        cost_estimate=COST,
        name=name,
    )(*own, *other, tied)


def shift(x, axis, by):
    n = lax.axis_size(axis)
    return lax.ppermute(x, axis, [(i, (i + by) % n) for i in range(n)])


def over_rows(x):
    return lax.all_to_all(x, ROWS, split_axis=0, concat_axis=0, tiled=True)


def after(x, *others):
    return lax.optimization_barrier((x, others))[0]


def turned(x):
    outer, inner, width = x.shape
    n = outer * inner
    to = lax.broadcasted_iota(jnp.int32, (n, n), 0)
    source = lax.broadcasted_iota(jnp.int32, (n, n), 1)
    turn = jnp.where(source == (to % outer) * inner + to // outer, 1.0, 0.0).astype(x.dtype)
    return nn(turn, x.reshape(n, width)).astype(x.dtype).reshape(inner, outer, width)


def column_pack_kernel(*refs):
    ins, o_ref = refs[:-1], refs[-1]
    groups, _, rows, _ = o_ref.shape
    for i, ref in enumerate(ins):
        for r in range(0, rows, groups):
            o_ref[:, i, r : r + groups] = turned(ref[r : r + groups])


def column_pack(arrays, pieces, groups):
    rows, _, features = arrays[0].shape
    n = len(arrays)
    return pl.pallas_call(
        column_pack_kernel,
        grid=(pieces,),
        in_specs=[pl.BlockSpec((rows, groups, features), lambda p: (0, p, 0))] * n,
        out_specs=pl.BlockSpec((groups, n, rows, features), lambda p: (0, p, 0, 0)),
        out_shape=jax.ShapeDtypeStruct((groups, n * pieces, rows, features), jnp.bfloat16),
        compiler_params=params(VMEM_ALL),
        cost_estimate=COST,
        name="column_pack",
    )(*arrays)


def column_unpack_kernel(x_ref, *o_refs):
    groups, _, rows, _ = x_ref.shape
    for i, ref in enumerate(o_refs):
        for r in range(0, rows, groups):
            ref[r : r + groups] = turned(x_ref[:, i, r : r + groups])


def column_unpack(x, pieces):
    groups, parts, rows, features = x.shape
    n = parts // pieces
    return pl.pallas_call(
        column_unpack_kernel,
        grid=(pieces,),
        in_specs=[pl.BlockSpec((groups, n, rows, features), lambda p: (0, p, 0, 0))],
        out_specs=[pl.BlockSpec((rows, groups, features), lambda p: (0, p, 0))] * n,
        out_shape=[jax.ShapeDtypeStruct((rows, pieces * groups, features), jnp.bfloat16)] * n,
        compiler_params=params(),
        cost_estimate=COST,
        name="column_unpack",
    )(x)


def local(row_query, row_key, row_value, row_out_grad, col_query, col_key, col_value, col_out_grad):
    groups = 1
    for axis in ROWS:
        groups *= lax.axis_size(axis)
    parts = lax.axis_size("x")
    here = lax.axis_index("x")
    rows, columns, features = row_query.shape
    row_factor = 1.0 / math.sqrt(HD * rows * groups)
    head_group = H // parts
    pieces = columns // groups

    def spread(chunks):
        return [chunks[0]] + [shift(chunks[s], "x", s) for s in range(1, parts)]

    here = jnp.reshape(here, (1,)).astype(jnp.int32)
    col_ready = column_pack((col_query, col_key, col_value, col_out_grad), pieces, groups)
    col_in = over_rows(col_ready)

    row_arrays = after((row_query, row_out_grad, row_key, row_value), col_ready)
    own = spread(pack_rows(here, parts, *row_arrays[:2]))
    keys = spread(pack_rows(here, parts, row_arrays[2]))
    values = spread(pack_rows(here, parts, row_arrays[3]))
    other = [shift(c, "yl", 1) for c in own]
    half = tied_terms(own, keys, values, groups, 0)
    col_done = column_backward(after(col_in, half), pieces)

    def across(keys, *others):
        return [shift(c, "yl", 1) for c in after(keys, others)]

    early = across([jnp.concatenate(keys[:2])], other[-2])[0]
    left, half = after((other[:-1], half), col_done)
    half = tied_terms(left, keys, values, groups, 1, 0, (half,))
    terms = over_rows(tied_terms(other[-1:], keys, values, groups, 1, parts - 1, (half,)))
    sums = jnp.sum(after(terms, early), axis=0)
    swapped = shift(sums, "yl", 1)
    late = across([jnp.concatenate(keys[2:])], swapped)[0]
    logits, dprobs = jnp.concatenate([sums, jnp.flip(swapped, 2)], axis=-1)
    probs = jax.nn.softmax(logits * row_factor, axis=-1)
    slopes = probs * (dprobs - jnp.sum(probs * dprobs, axis=-1, keepdims=True))
    probs, slopes = probs.astype(jnp.bfloat16), slopes.astype(jnp.bfloat16)
    wide = probs.shape[-1] // 2
    payload = jnp.stack(
        [
            slopes[:, 0, :, :wide],
            probs[:, 0, :, :wide],
            slopes[:, 0, :, wide:],
            slopes[:, 1, :, :wide],
            probs[:, 1, :, :wide],
        ]
    )
    whole = over_rows(jnp.broadcast_to(payload[None], (groups,) + payload.shape))
    whole = jnp.transpose(whole, (1, 2, 0, 3, 4)).reshape(5, head_group, wide, wide)
    def back(chunks):
        return [chunks[0]] + [shift(chunks[s], "x", parts - s) for s in range(1, parts)]

    pair_grads = tied_grads(pair_grads_kernel, own, other, whole, row_factor, "pair_grads")
    key_chunks, value_chunks = back(pair_grads[:parts]), back(pair_grads[parts:])
    col_grads = column_unpack(over_rows(after(col_done, whole, late)), pieces)
    keys = after(keys, value_chunks[1])
    query_grads = tied_grads(query_grads_kernel, keys, [early, late], whole, row_factor, "query_grads")
    chunks = (back(query_grads), key_chunks, value_chunks)
    row_grads = [unpack_rows(here, c)[0] for c in chunks[1:]]
    row_grads.insert(0, unpack_rows(here, after(chunks[0], col_grads))[0])

    return (*row_grads, *col_grads)


def solution(mesh):
    split = Mesh(mesh.devices.reshape(4, 2, 2, 2, 4), ("z", "yh", "core", "yl", "x"))
    spec = P(ROWS, ("yl", "x"), None)
    return jax.shard_map(
        local, mesh=split, in_specs=(spec,) * 8, out_specs=(spec,) * 6, check_vma=False
    )
```

```python
import functools
import math

import jax
import jax.numpy as jnp
from jax import lax
from jax.experimental import pallas as pl
from jax.experimental.pallas import tpu as pltpu
from jax.sharding import Mesh
from jax.sharding import PartitionSpec as P

H = 12
HD = 64
PAIR = 2 * HD
LOG2E = 1.4426950408889634
ROWS = ("z", "yh", "core")
VMEM = 48 * 1024 * 1024
VMEM_ALL = 60 * 1024 * 1024
COST = pl.CostEstimate(flops=1, bytes_accessed=1, transcendentals=0)


def params(limit=VMEM):
    return pltpu.CompilerParams(vmem_limit_bytes=limit)


def nt(a, b):
    return lax.dot_general(a, b, (((1,), (1,)), ((), ())), preferred_element_type=jnp.float32)


def nn(a, b):
    return lax.dot_general(a, b, (((1,), (0,)), ((), ())), preferred_element_type=jnp.float32)


def tn(a, b):
    return lax.dot_general(a, b, (((0,), (0,)), ((), ())), preferred_element_type=jnp.float32)


def column_kernel(x_ref, o_ref, *, chunk):
    groups, _, rows, width = x_ref.shape
    total = groups * rows
    query, key, value, grad = (x_ref[:, i].reshape(total, width) for i in range(4))
    low = lax.broadcasted_iota(jnp.int32, (total, width), 1) < HD
    zero = jnp.zeros_like(key)
    key_t = key.T
    scale = 1.0 / math.sqrt(HD)
    key_grads, value_grads, query_grads = [], [], []
    for head in range(2):
        keep = low if head == 0 else jnp.logical_not(low)
        key_h = jnp.where(keep, key, zero)
        value_h = jnp.where(keep, value, zero)
        key_th = key_t[head * HD : (head + 1) * HD]
        key_grad, value_grad, parts = None, None, []
        for at in range(0, total, chunk):
            query_c, grad_c = query[at : at + chunk], grad[at : at + chunk]
            logits = nt(key_h, query_c)
            dprobs = nt(value_h, grad_c)
            top = jnp.max(logits, axis=0, keepdims=True)
            probs = jnp.exp2((logits - top) * (scale * LOG2E))
            probs = probs * (1.0 / jnp.sum(probs, axis=0, keepdims=True))
            slopes = probs * (dprobs - jnp.sum(probs * dprobs, axis=0, keepdims=True))
            weights = probs.astype(jnp.bfloat16)
            slopes = slopes.astype(jnp.bfloat16)
            more_key, more_value = nn(slopes, query_c), nn(weights, grad_c)
            key_grad = more_key if key_grad is None else key_grad + more_key
            value_grad = more_value if value_grad is None else value_grad + more_value
            parts.append(nn(key_th, slopes))
        key_grads.append(key_grad)
        value_grads.append(value_grad)
        query_grads.append(jnp.concatenate(parts, axis=1))
    query_grad = jnp.concatenate(query_grads, axis=0).T * scale
    key_grad = jnp.where(low, key_grads[0], key_grads[1]) * scale
    value_grad = jnp.where(low, value_grads[0], value_grads[1])
    for i, grad in enumerate((query_grad, key_grad, value_grad)):
        o_ref[:, i] = grad.astype(jnp.bfloat16).reshape(groups, rows, width)


def column_backward(x, pieces, chunk=512):
    groups, _, rows, features = x.shape
    pairs, total = features // PAIR, groups * rows
    return pl.pallas_call(
        functools.partial(column_kernel, chunk=chunk),
        grid=(pieces, pairs),
        in_specs=[pl.BlockSpec((groups, 4, rows, PAIR), lambda p, i: (0, p, 0, i))],
        out_specs=pl.BlockSpec((groups, 3, rows, PAIR), lambda p, i: (0, p, 0, i)),
        out_shape=jax.ShapeDtypeStruct((groups, 3 * pieces, rows, features), jnp.bfloat16),
        compiler_params=params(),
        cost_estimate=pl.CostEstimate(
            flops=20 * pieces * pairs * total * total * PAIR,
            bytes_accessed=14 * pieces * total * features,
            transcendentals=2 * pieces * pairs * total * total,
        ),
        name="column_attention",
    )(x)


def pack_kernel(here_ref, *refs, parts):
    ins, outs, held, sems = refs[: -parts - 2], refs[-parts - 2 : -2], refs[-2], refs[-1]
    group = held.shape[1]
    for t in range(parts):
        for k in range(group):
            lanes = slice((t * group + k) * HD, (t * group + k + 1) * HD)
            for i, ref in enumerate(ins):
                for r in range(0, ref.shape[0], 2):
                    held[t, k, i, :, r * HD : r * HD + PAIR] = jnp.concatenate(
                        [ref[r, :, lanes], ref[r + 1, :, lanes]], axis=1
                    )
        for s, out in enumerate(outs):

            @pl.when(lax.rem(t + parts - here_ref[0], parts) == s)
            def _(t=t, out=out):
                pltpu.make_async_copy(held.at[t], out, sems.at[t]).start()

    for t in range(parts):
        pltpu.make_async_copy(held.at[t], outs[0], sems.at[t]).wait()


def pack_rows(here, parts, *arrays):
    rows, columns, features = arrays[0].shape
    n, group = len(arrays), features // HD // parts
    shape = (group, n, columns, rows * HD)
    return pl.pallas_call(
        functools.partial(pack_kernel, parts=parts),
        in_specs=[pl.BlockSpec(memory_space=pltpu.SMEM)]
        + [pl.BlockSpec(memory_space=pltpu.VMEM)] * n,
        out_specs=[pl.BlockSpec(memory_space=pl.ANY)] * parts,
        out_shape=[jax.ShapeDtypeStruct(shape, jnp.bfloat16)] * parts,
        scratch_shapes=[
            pltpu.VMEM((parts,) + shape, jnp.bfloat16),
            pltpu.SemaphoreType.DMA((parts,)),
        ],
        compiler_params=params(),
        cost_estimate=COST,
        name="pack_rows",
    )(here, *arrays)


def unpack_kernel(here_ref, *refs, parts):
    ins, o_refs, held, sems = refs[:parts], refs[parts:-2], refs[-2], refs[-1]
    group = held.shape[1]
    for t in range(parts):
        for s, ref in enumerate(ins):

            @pl.when(lax.rem(t + parts - here_ref[0], parts) == s)
            def _(t=t, ref=ref):
                pltpu.make_async_copy(ref, held.at[t], sems.at[t]).start()

    for t in range(parts):
        pltpu.make_async_copy(ins[0], held.at[t], sems.at[t]).wait()
    for head in range(0, parts * group, 2):
        lanes = slice(head * HD, head * HD + PAIR)
        even, odd = divmod(head, group), divmod(head + 1, group)
        for i, ref in enumerate(o_refs):
            for r in range(0, ref.shape[0], 2):
                span = slice(r * HD, r * HD + PAIR)
                first, second = held[*even, i, :, span], held[*odd, i, :, span]
                ref[r, :, lanes] = jnp.concatenate([first[:, :HD], second[:, :HD]], axis=1)
                ref[r + 1, :, lanes] = jnp.concatenate([first[:, HD:], second[:, HD:]], axis=1)


def unpack_rows(here, chunks):
    parts = len(chunks)
    group, n, columns, width = chunks[0].shape
    rows, features = width // HD, parts * group * HD
    return pl.pallas_call(
        functools.partial(unpack_kernel, parts=parts),
        in_specs=[pl.BlockSpec(memory_space=pltpu.SMEM)]
        + [pl.BlockSpec(memory_space=pl.ANY)] * parts,
        out_specs=[pl.BlockSpec(memory_space=pltpu.VMEM)] * n,
        out_shape=[jax.ShapeDtypeStruct((rows, columns, features), jnp.bfloat16)] * n,
        scratch_shapes=[
            pltpu.VMEM((parts,) + chunks[0].shape, jnp.bfloat16),
            pltpu.SemaphoreType.DMA((parts,)),
        ],
        compiler_params=params(),
        cost_estimate=COST,
        name="unpack_rows",
    )(here, *chunks)


def joined(refs, i):
    return jnp.concatenate([ref[0, i] for ref in refs], axis=0)


def terms_kernel(*refs, count, parts):
    left, keys, values = refs[:count], refs[count : count + parts], refs[count + parts :][:parts]
    o_ref = refs[-1]
    for i, right in enumerate((keys, values)):
        terms = nt(joined(left, i), joined(right, 0))
        o_ref[:, i, 0, 0] = terms.reshape(o_ref.shape[0], -1, terms.shape[1])


def tied_terms(left, keys, values, slices, side, first=0, held=()):
    parts, count = len(keys), len(left)
    heads, _, columns, width = left[0].shape
    wide = parts * columns
    step, span = wide // slices, slices * count // parts
    return pl.pallas_call(
        functools.partial(terms_kernel, count=count, parts=parts),
        grid=(heads,),
        in_specs=[pl.BlockSpec((1, 2, columns, width), lambda i: (i, 0, 0, 0))] * count
        + [pl.BlockSpec((1, 1, columns, width), lambda i: (i, 0, 0, 0))] * (2 * parts)
        + [pl.BlockSpec(memory_space=pl.ANY)] * len(held),
        out_specs=pl.BlockSpec(
            (span, 2, 1, 1, step, wide), lambda i: (first // count, 0, i, side, 0, 0)
        ),
        out_shape=jax.ShapeDtypeStruct((slices, 2, heads, 2, step, wide), jnp.float32),
        input_output_aliases={count + 2 * parts: 0} if held else {},
        compiler_params=params(),
        cost_estimate=COST,
        name="tied_terms",
    )(*left, *keys, *values, *held)


def pair_grads_kernel(*refs, parts, factor):
    own, other, (tied_ref, *outs) = refs[:parts], refs[parts : 2 * parts], refs[2 * parts :]
    s_own, w_own, _, s_below, w_below = (tied_ref[i, 0] for i in range(5))
    s_key = jnp.concatenate([s_own, s_below], axis=0)
    w_value = jnp.concatenate([w_own, w_below], axis=0)
    results = (
        tn(s_key, jnp.concatenate([joined(own, 0), joined(other, 0)], axis=0)) * factor,
        tn(w_value, jnp.concatenate([joined(own, 1), joined(other, 1)], axis=0)),
    )
    for i, result in enumerate(results):
        result = result.astype(jnp.bfloat16)
        for s, out in enumerate(outs[i * parts : (i + 1) * parts]):
            out[0, 0] = result[s * out.shape[2] : (s + 1) * out.shape[2]]


def query_grads_kernel(*refs, parts, factor):
    keys, other_keys, (tied_ref, *outs) = refs[:parts], refs[parts : 2 * parts], refs[2 * parts :]
    s_query = jnp.concatenate([tied_ref[0, 0], tied_ref[2, 0]], axis=1)
    result = nn(s_query, jnp.concatenate([joined(keys, 0), joined(other_keys, 0)], axis=0))
    result = (result * factor).astype(jnp.bfloat16)
    for s, out in enumerate(outs):
        out[0, 0] = result[s * out.shape[2] : (s + 1) * out.shape[2]]


def tied_grads(kernel, own, other, tied, factor, name):
    parts = len(own)
    heads, n, columns, width = own[0].shape
    places = [
        pl.BlockSpec((1, n, columns, width), lambda i, at=at: (at + i, 0, 0, 0))
        for x in other
        for at in range(0, x.shape[0], heads)
    ]
    other = [x for x in other for _ in range(0, x.shape[0], heads)]
    wide = parts * columns
    chunk = pl.BlockSpec((1, n, columns, width), lambda i: (i, 0, 0, 0))
    one = pl.BlockSpec((1, 1, columns, width), lambda i: (i, 0, 0, 0))
    square = pl.BlockSpec((5, 1, wide, wide), lambda i: (0, i, 0, 0))
    return pl.pallas_call(
        functools.partial(kernel, parts=parts, factor=factor),
        grid=(heads,),
        in_specs=[chunk] * parts + places + [square],
        out_specs=[one] * (n * parts),
        out_shape=[jax.ShapeDtypeStruct((heads, 1, columns, width), jnp.bfloat16)] * (n * parts),
        compiler_params=params(VMEM_ALL),
        cost_estimate=COST,
        name=name,
    )(*own, *other, tied)


def shift(x, axis, by):
    n = lax.axis_size(axis)
    return lax.ppermute(x, axis, [(i, (i + by) % n) for i in range(n)])


def over_rows(x):
    return lax.all_to_all(x, ROWS, split_axis=0, concat_axis=0, tiled=True)


def after(x, *others):
    return lax.optimization_barrier((x, others))[0]


def turned(x):
    outer, inner, width = x.shape
    n = outer * inner
    to = lax.broadcasted_iota(jnp.int32, (n, n), 0)
    source = lax.broadcasted_iota(jnp.int32, (n, n), 1)
    turn = jnp.where(source == (to % outer) * inner + to // outer, 1.0, 0.0).astype(x.dtype)
    return nn(turn, x.reshape(n, width)).astype(x.dtype).reshape(inner, outer, width)


def column_pack_kernel(*refs):
    ins, o_ref = refs[:-1], refs[-1]
    groups, _, rows, _ = o_ref.shape
    for i, ref in enumerate(ins):
        for r in range(0, rows, groups):
            o_ref[:, i, r : r + groups] = turned(ref[r : r + groups])


def column_pack(arrays, pieces, groups):
    rows, _, features = arrays[0].shape
    n = len(arrays)
    return pl.pallas_call(
        column_pack_kernel,
        grid=(pieces,),
        in_specs=[pl.BlockSpec((rows, groups, features), lambda p: (0, p, 0))] * n,
        out_specs=pl.BlockSpec((groups, n, rows, features), lambda p: (0, p, 0, 0)),
        out_shape=jax.ShapeDtypeStruct((groups, n * pieces, rows, features), jnp.bfloat16),
        compiler_params=params(VMEM_ALL),
        cost_estimate=COST,
        name="column_pack",
    )(*arrays)


def column_unpack_kernel(x_ref, *o_refs):
    groups, _, rows, _ = x_ref.shape
    for i, ref in enumerate(o_refs):
        for r in range(0, rows, groups):
            ref[r : r + groups] = turned(x_ref[:, i, r : r + groups])


def column_unpack(x, pieces):
    groups, parts, rows, features = x.shape
    n = parts // pieces
    return pl.pallas_call(
        column_unpack_kernel,
        grid=(pieces,),
        in_specs=[pl.BlockSpec((groups, n, rows, features), lambda p: (0, p, 0, 0))],
        out_specs=[pl.BlockSpec((rows, groups, features), lambda p: (0, p, 0))] * n,
        out_shape=[jax.ShapeDtypeStruct((rows, pieces * groups, features), jnp.bfloat16)] * n,
        compiler_params=params(),
        cost_estimate=COST,
        name="column_unpack",
    )(x)


def local(row_query, row_key, row_value, row_out_grad, col_query, col_key, col_value, col_out_grad):
    groups = 1
    for axis in ROWS:
        groups *= lax.axis_size(axis)
    parts = lax.axis_size("x")
    here = lax.axis_index("x")
    rows, columns, features = row_query.shape
    row_factor = 1.0 / math.sqrt(HD * rows * groups)
    head_group = H // parts
    pieces = columns // groups

    def spread(chunks):
        return [chunks[0]] + [shift(chunks[s], "x", s) for s in range(1, parts)]

    here = jnp.reshape(here, (1,)).astype(jnp.int32)
    col_ready = column_pack((col_query, col_key, col_value, col_out_grad), pieces, groups)
    col_in = over_rows(col_ready)

    row_arrays = after((row_query, row_out_grad, row_key, row_value), col_ready)
    own = spread(pack_rows(here, parts, *row_arrays[:2]))
    keys = spread(pack_rows(here, parts, row_arrays[2]))
    values = spread(pack_rows(here, parts, row_arrays[3]))
    other = [shift(c, "yl", 1) for c in own]
    half = tied_terms(own, keys, values, groups, 0)
    col_done = column_backward(after(col_in, half), pieces)

    def across(keys, *others):
        return [shift(c, "yl", 1) for c in after(keys, others)]

    early = across([jnp.concatenate(keys[:2])], other[-2])[0]
    left, half = after((other[:-1], half), col_done)
    half = tied_terms(left, keys, values, groups, 1, 0, (half,))
    terms = over_rows(tied_terms(other[-1:], keys, values, groups, 1, parts - 1, (half,)))
    sums = jnp.sum(after(terms, early), axis=0)
    swapped = shift(sums, "yl", 1)
    late = across([jnp.concatenate(keys[2:])], swapped)[0]
    logits, dprobs = jnp.concatenate([sums, jnp.flip(swapped, 2)], axis=-1)
    probs = jax.nn.softmax(logits * row_factor, axis=-1)
    slopes = probs * (dprobs - jnp.sum(probs * dprobs, axis=-1, keepdims=True))
    probs, slopes = probs.astype(jnp.bfloat16), slopes.astype(jnp.bfloat16)
    wide = probs.shape[-1] // 2
    payload = jnp.stack(
        [
            slopes[:, 0, :, :wide],
            probs[:, 0, :, :wide],
            slopes[:, 0, :, wide:],
            slopes[:, 1, :, :wide],
            probs[:, 1, :, :wide],
        ]
    )
    whole = over_rows(jnp.broadcast_to(payload[None], (groups,) + payload.shape))
    whole = jnp.transpose(whole, (1, 2, 0, 3, 4)).reshape(5, head_group, wide, wide)
    def back(chunks):
        return [chunks[0]] + [shift(chunks[s], "x", parts - s) for s in range(1, parts)]

    pair_grads = tied_grads(pair_grads_kernel, own, other, whole, row_factor, "pair_grads")
    key_chunks, value_chunks = back(pair_grads[:parts]), back(pair_grads[parts:])
    col_grads = column_unpack(over_rows(after(col_done, whole, late)), pieces)
    keys = after(keys, value_chunks[1])
    query_grads = tied_grads(query_grads_kernel, keys, [early, late], whole, row_factor, "query_grads")
    chunks = (back(query_grads), key_chunks, value_chunks)
    row_grads = [unpack_rows(here, c)[0] for c in chunks[1:]]
    row_grads.insert(0, unpack_rows(here, after(chunks[0], col_grads))[0])

    return (*row_grads, *col_grads)


def solution(mesh):
    split = Mesh(mesh.devices.reshape(4, 2, 2, 2, 4), ("z", "yh", "core", "yl", "x"))
    spec = P(ROWS, ("yl", "x"), None)
    return jax.shard_map(
        local, mesh=split, in_specs=(spec,) * 8, out_specs=(spec,) * 6, check_vma=False
    )
```
